128 devices in a mesh: prompt: 8 (over z, y_lo), ctx: 16 (over x, y_hi, core).
Axes of the slice: x: 4, y: 4 (y_hi: 2, y_lo: 2; y = y_hi * 2 + y_lo), z: 4, core: 2. Of those that a mesh axis runs over, the one named last changes fastest.
Arguments:
- query_latent: bfloat16 [8, 3072, 1536], P('prompt', 'ctx'), may hold values from -41 to 41
- kv_latent: bfloat16 [8, 3072, 576], P('prompt', 'ctx'), may hold values from -6 to 6
- query_up: bfloat16 [1536, 3072], replicated, may hold values from -0.15625 to 0.15625
- key_absorb: bfloat16 [16, 128, 512], replicated, may hold values from -0.5 to 0.5
- value_up_weight: bfloat16 [16, 512, 128], replicated, may hold values from -0.25 to 0.25
- block_order: int32 [8, 32], P('prompt', 'ctx'), may hold values from 0 to 31, each once within a row
- page_owner: int32 [8, 192, 1], P('prompt', 'ctx'), may hold values from 0 to 7; in each aligned block of 12 rows (0 to 11, 12 to 23, ..., all dimensions but the last counted through in order) at most 3 rows name the same one
Outputs:
- attention_out: bfloat16 [8, 3072, 2048], P('prompt', 'ctx')
- cache_pages: bfloat16 [8, 16, 8, 3, 9216], P('prompt', 'ctx')
- page_start: int32 [8, 16, 8, 3], P('prompt', 'ctx')
The draws below stay inside these ranges and needn't reach their ends.
Inputs may be any that keep to these rules, and one draw needn't show every extreme that they name: `block_order`: each prompt's row names every block of 96 positions once. `page_owner`: among the 12 pages of one device at most 3 have the same owner.
All inputs are finite; a program needn't handle non-finite values.
Results may differ from the reference program's by a relative error of at most 0.015.
The reference program's roundings to bfloat16 on the way count: a program that leaves them out, or rounds other values in their place, can miss the bound.
Values may be sent and summed in bfloat16 or wider, within the bound.
No kernel may reach another device: no remote copies, remote signals or barrier semaphores. Data moves between devices by JAX's collectives and lax.ppermute only.
A program may use at most 128 MiB of HBM per device.

```python
import math
import jax
import jax.numpy as jnp
import numpy as np
from jax import lax

QL = 1536
KVR = 512
NOPE = 128
ROPE = 64
VD = 128
H = 16
PAGE = 16
TOK_DEV = 192
HALF = 96
SEQ = 3072
PROMPTS = 8
LAT = 576
QKD = 192
PAGES_DEV = 12
SEND_CAP = 3
N_CTX = 16


def draw_query_latent(key, part):
    key = jax.random.fold_in(key, 7)
    first_key = jax.random.fold_in(key, 0)
    base = jnp.clip(jax.random.normal(first_key, (PROMPTS, SEQ, QL), jnp.float32), -6.0, 6.0)
    return base.astype(jnp.bfloat16)


def steps_of(rng, dims, cuts, least, top_value):
    level = 1.0
    for position, parts in cuts:
        draws = jax.random.uniform(jax.random.fold_in(jax.random.fold_in(rng, 6), position), (parts,), jnp.float32, least / len(cuts), top_value / len(cuts))
        level = level * jnp.repeat(jnp.exp(draws), dims[position] // parts).reshape((-1,) + (1,) * (len(dims) - 1 - position))
    return level


def routed_block(key, own, number, rows, count, top, most, lean):
    ranking = jax.random.permutation(key, count)
    packed, ordinary = load_shares(count, rows * top, most, lean, True), load_shares(count, rows * top, most, lean, False)
    places = jnp.arange(count)

    def named(sizes, offset_by):
        used = int((sizes > 0).sum())
        fixed = max(1, used // 4)
        moved = fixed + (places - fixed + offset_by * (used - fixed)) % max(1, count - fixed)
        return jnp.zeros((count,), jnp.int32).at[ranking[jnp.where(places < fixed, places, moved)]].set(jnp.asarray(sizes, jnp.int32))

    sizes = jnp.where(number % 4 == 0, named(packed, number // 4), named(ordinary, number - number // 4 - 1))
    mixed = jax.random.permutation(jax.random.fold_in(own, 3), count)
    donor, taker = mixed[0:count // 2 * 2:2], mixed[1:count // 2 * 2:2]
    room = jnp.minimum(sizes[donor] - 1, most - sizes[taker]) // 2
    room = jnp.where((donor == ranking[0]) | (taker == ranking[0]) | (sizes[taker] == 0), 0, jnp.maximum(room, 0))
    moved = jax.random.randint(jax.random.fold_in(own, 4), (count // 2,), 0, 1 << 20) % (room + 1)
    sizes = sizes.at[donor].add(-moved).at[taker].add(moved)
    items = jnp.searchsorted(jnp.cumsum(sizes), jnp.arange(rows * top), side="right").astype(jnp.int32)
    grid = items.reshape(top, rows).T
    grid = grid[jax.random.permutation(jax.random.fold_in(own, 1), rows)]
    offset_by = jax.random.randint(jax.random.fold_in(own, 2), (rows, 1), 0, top)
    return jnp.take_along_axis(grid, (jnp.arange(top)[None, :] + offset_by) % top, axis=1)


def load_shares(count, total, bound, lean, full):
    loads = [(1 << 20) // math.isqrt(grade ** lean) + 1 for grade in range(1, count + 1)]
    largest = bound if full else min(bound, max(-(-total // count), total * loads[0] // sum(loads)))
    least = 1 if total - largest >= count - 1 else 0
    given, surplus = [largest] + [least] * (count - 1), total - largest - least * (count - 1)
    while surplus > 0:
        free = [i for i in range(1, count) if given[i] < largest] or [i for i in range(1, count) if given[i] < bound]
        whole, remaining = sum([loads[i] for i in free]), surplus
        for i in free:
            extra = min(bound - given[i], max(1, remaining * loads[i] // whole), surplus)
            given[i] = given[i] + extra
            surplus = surplus - extra
    return np.array(given)


def gaussian(stream_key, dims, deviation, bound, shards=(), kind=jnp.bfloat16):
    drawn = jax.random.normal(stream_key, dims, jnp.float32) * deviation
    if len(shards) > 0:
        drawn = steps_of(stream_key, dims, shards, -0.22, 0.18) * drawn
    return jnp.clip(drawn, min=-bound, max=bound).astype(kind)


def setup_inputs(seed: int = 0) -> dict:
    seeds = jax.random.split(jax.random.key(seed), 8)
    query_latent = draw_query_latent(jax.random.fold_in(seeds[7], 71), 0)
    kv_latent = gaussian(seeds[1], (PROMPTS, SEQ, LAT), 1.0, 6.0, ((0, 8), (1, 16)))
    query_up = gaussian(seeds[2], (QL, H * QKD), QL ** -0.5, 0.15625)
    key_absorb = gaussian(seeds[3], (H, NOPE, KVR), NOPE ** -0.5, 0.5)
    value_up_weight = gaussian(seeds[4], (H, KVR, VD), KVR ** -0.5, 0.25)
    block_order = jax.vmap(lambda own: jax.random.permutation(own, 2 * N_CTX))(jax.random.split(seeds[5], PROMPTS)).reshape((PROMPTS, 2 * N_CTX)).astype(jnp.int32)
    page_owner_keys = jax.random.split(jax.random.fold_in(seeds[6], 1), PROMPTS * (N_CTX * PAGES_DEV) // PAGES_DEV)
    page_owner_turns = jax.random.permutation(jax.random.fold_in(seeds[6], 3), PROMPTS * (N_CTX * PAGES_DEV) // PAGES_DEV)
    page_owner = jax.vmap(lambda own, number: routed_block(jax.random.fold_in(seeds[6], 2), own, number, PAGES_DEV, PROMPTS, 1, SEND_CAP, 1))(page_owner_keys, page_owner_turns).reshape((PROMPTS, N_CTX * PAGES_DEV, 1))
    return dict(query_latent=query_latent, kv_latent=kv_latent, query_up=query_up, key_absorb=key_absorb, value_up_weight=value_up_weight, block_order=block_order, page_owner=page_owner)


ROPE_BASE = 10000.0


def rotate(pe_part, positions):
    half_dim = pe_part.shape[-1] // 2
    inverse = ROPE_BASE ** (-2.0 * jnp.arange(half_dim, dtype=jnp.float32) / pe_part.shape[-1])
    angles = positions.astype(jnp.float32)[:, None, None] * inverse
    cosine = jnp.cos(angles)
    sine = jnp.sin(angles)
    first = pe_part[..., :half_dim]
    second = pe_part[..., half_dim:]
    return jnp.concatenate([first * cosine - second * sine, first * sine + second * cosine], axis=-1)


def queries(query_rows, positions, query_up, key_absorb):
    row_count = query_rows.shape[0]
    head_count = key_absorb.shape[0]
    nope_dim = key_absorb.shape[1]
    projected = jnp.dot(query_rows, query_up, preferred_element_type=jnp.float32).astype(jnp.bfloat16)
    projected = projected.reshape(row_count, head_count, -1)
    absorbed = jnp.einsum("shn,hnk->shk", projected[..., :nope_dim].astype(jnp.float32), key_absorb.astype(jnp.float32))
    rotated = rotate(projected[..., nope_dim:].astype(jnp.float32), positions)
    return jnp.concatenate([absorbed, rotated], axis=-1).astype(jnp.bfloat16)


def reference(query_latent, kv_latent, query_up, key_absorb, value_up_weight, block_order, page_owner):
    scale_factor = (NOPE + ROPE) ** -0.5
    row_index = jnp.arange(SEQ, dtype=jnp.int32)
    device_of = row_index // TOK_DEV
    local_row = row_index % TOK_DEV

    def one_prompt(inputs):
        query_rows, latent_rows, order_row = inputs
        positions = order_row[device_of * 2 + local_row // HALF] * HALF + local_row % HALF
        query_full = queries(query_rows, positions, query_up, key_absorb)
        values = latent_rows[:, :KVR]
        visible = positions[None, :] <= positions[:, None]

        def one_head(head_rows):
            scores = jnp.dot(head_rows, latent_rows.T, preferred_element_type=jnp.float32) * scale_factor
            scores = jnp.where(visible, scores, -jnp.inf)
            weights = jax.nn.softmax(scores, axis=-1).astype(jnp.bfloat16)
            return jnp.dot(weights, values, preferred_element_type=jnp.float32).astype(jnp.bfloat16)

        latent_output_rows = lax.map(one_head, jnp.transpose(query_full, (1, 0, 2)))
        final_output = jnp.einsum("fue,feq->ufq", latent_output_rows.astype(jnp.float32), value_up_weight.astype(jnp.float32))
        return final_output.astype(jnp.bfloat16).reshape(SEQ, H * VD)

    attention_out = lax.map(one_prompt, (query_latent, kv_latent, block_order))

    latent_page_list = kv_latent.reshape(PROMPTS, N_CTX, PAGES_DEV, PAGE * LAT)
    owners = page_owner.reshape(PROMPTS, N_CTX, PAGES_DEV)
    onehot = (owners[..., None] == jnp.arange(PROMPTS, dtype=jnp.int32)).astype(jnp.int32)
    slot_rank = jnp.sum((jnp.cumsum(onehot, axis=2) - onehot) * onehot, axis=-1)
    target_slot = owners * SEND_CAP + slot_rank
    page_selector = (target_slot[..., None] == jnp.arange(PROMPTS * SEND_CAP, dtype=jnp.int32)).astype(jnp.int32)
    moved_pages = jnp.einsum("jkub,jkul->bkjl", page_selector.astype(jnp.float32), latent_page_list.astype(jnp.float32))
    moved_pages = moved_pages.reshape(PROMPTS, SEND_CAP, N_CTX, PROMPTS, PAGE * LAT)
    cache_pages = jnp.transpose(moved_pages, (0, 2, 3, 1, 4)).astype(jnp.bfloat16)
    page_local = jnp.arange(PAGES_DEV, dtype=jnp.int32) * PAGE
    slot_blocks = block_order.reshape(PROMPTS, N_CTX, 2)[:, :, page_local // HALF]
    starts = slot_blocks * HALF + page_local % HALF
    start_slots = jnp.sum(page_selector * (starts + 1)[..., None], axis=2) - 1
    start_slots = start_slots.reshape(PROMPTS, N_CTX, PROMPTS, SEND_CAP)
    page_start = jnp.transpose(start_slots, (2, 1, 0, 3)).astype(jnp.int32)
    return attention_out, cache_pages, page_start
```

```python
import functools
import math

import jax
import jax.numpy as jnp
import numpy as np
from jax import lax
from jax.experimental import pallas as pl
from jax.experimental.pallas import tpu as pltpu
from jax.sharding import PartitionSpec as P

F32 = jnp.float32
BF16 = jnp.bfloat16
NOPE, ROPE, KVR, VD, HEADS = 128, 64, 512, 128, 16
LAT = KVR + ROPE
WIDE = 640
PAGE, PAGES, CAP = 16, 12, 3
HALF, ROWS = 96, 192
BLOCKS = 32
FLAT = PAGE * LAT
META = FLAT + 128
BIG = 1e30
SCALE2 = (NOPE + ROPE) ** -0.5 * math.log2(math.e)
VMEM_LIMIT = 48 * 2**20


def rope_tables():
    lane = np.arange(128)
    freq = 10000.0 ** (-2.0 * (lane % 32) / ROPE)
    sign = np.where(lane % 64 < 32, -1.0, 1.0)

    def table(places):
        angle = places[:, None] * freq
        return np.concatenate([np.cos(angle), sign * np.sin(angle)], axis=1).astype(np.float32)

    return table(np.arange(BLOCKS) * float(HALF)), table(np.arange(HALF) * 1.0)


def query_kernel(blk, ql, qu, ka, block_table, offset_table, out, rope_s, ext_s):
    lane = lax.broadcasted_iota(jnp.int32, (ROWS, 128), 1)

    @pl.when(pl.program_id(0) == 0)
    def _():
        half_lane = lax.broadcasted_iota(jnp.int32, (HALF, 128), 1)
        for slot in range(2):
            here = blk[0, slot]
            base = block_table[pl.ds(here, 1), :]
            bc, bs = base[:, :128], base[:, 128:]
            oc, os = offset_table[:, :128], offset_table[:, 128:]
            rows = slice(slot * HALF, (slot + 1) * HALF)
            rope_s[rows, :128] = bc * oc - bs * os
            rope_s[rows, 128:] = bs * oc + bc * os
            later = (half_lane >= 64 + here + 1) & (half_lane < 64 + BLOCKS)
            ext_s[rows, :] = jnp.where(later, -BIG, 0.0)

    low = lane < 64
    both = jnp.dot(ql[...], qu[...], preferred_element_type=F32).astype(BF16)
    t0 = both[:, :128]
    t1 = both[:, 128:256].astype(F32)
    t2 = both[:, 256:].astype(F32)
    odd = jnp.where(low, t2, t1).astype(BF16)
    pair = jnp.where(low, t1, t2)
    swapped = jnp.where(lane % 64 < 32, pltpu.roll(pair, 96, 1), pltpu.roll(pair, 32, 1))
    turned = pair * rope_s[:, :128] + swapped * rope_s[:, 128:]
    out[0, :, :KVR] = jnp.dot(t0, ka[0], preferred_element_type=F32).astype(BF16)
    swapped_key = jnp.concatenate([ka[1, 64:, :], ka[1, :64, :]], axis=0)
    out[1, :, :KVR] = jnp.dot(odd, swapped_key, preferred_element_type=F32).astype(BF16)
    out[0, :, KVR:] = jnp.where(low, turned, ext_s[...]).astype(BF16)
    out[1, :, KVR:] = jnp.where(low, pltpu.roll(turned, 64, 1), ext_s[...]).astype(BF16)


def queries(blk, ql, qu, ka):
    block_table, offset_table = rope_tables()
    whole = lambda i, blk: (0, 0)
    return pl.pallas_call(
        query_kernel,
        grid_spec=pltpu.PrefetchScalarGridSpec(
            num_scalar_prefetch=1,
            grid=(HEADS // 2,),
            in_specs=[
                pl.BlockSpec((ROWS, ql.shape[1]), whole),
                pl.BlockSpec((qu.shape[0], 384), lambda i, blk: (0, i)),
                pl.BlockSpec((2, NOPE, KVR), lambda i, blk: (i, 0, 0)),
                pl.BlockSpec((BLOCKS, 256), whole),
                pl.BlockSpec((HALF, 256), whole),
            ],
            out_specs=pl.BlockSpec((2, ROWS, WIDE), lambda i, blk: (i, 0, 0)),
            scratch_shapes=[pltpu.VMEM((ROWS, 256), F32), pltpu.VMEM((ROWS, 128), F32)],
        ),
        out_shape=jax.ShapeDtypeStruct((HEADS, ROWS, WIDE), BF16),
        compiler_params=pltpu.CompilerParams(vmem_limit_bytes=VMEM_LIMIT),
        cost_estimate=pl.CostEstimate(
            flops=int(2.6e9), bytes_accessed=int(15e6), transcendentals=0
        ),
        name="queries",
    )(blk, ql, qu, ka, jnp.asarray(block_table), jnp.asarray(offset_table))


def attend_kernel(count, group, first, last, *refs):
    refs = list(refs)
    q_ref = refs.pop(0)
    pieces = [refs.pop(0) for _ in range(count)]
    if not first:
        stat_in, acc_in = refs.pop(0), refs.pop(0)
    if last:
        up_ref, out_ref = refs.pop(0), refs.pop(0)
    else:
        stat_out, acc_out = refs.pop(0), refs.pop(0)
    keys = refs.pop(0)
    mask = refs.pop(0) if first else None
    pair = 2
    rows = pair * ROWS

    @pl.when(pl.program_id(0) == 0)
    def _():
        for i in range(count):
            keys[i * ROWS : (i + 1) * ROWS, :] = pieces[i][...]
        if first:
            r = lax.broadcasted_iota(jnp.int32, (ROWS, 256), 0)
            t = lax.broadcasted_iota(jnp.int32, (ROWS, 256), 1)
            same = ((r < HALF) & (t < HALF)) | ((r >= HALF) & (t >= HALF) & (t < ROWS))
            mask[...] = jnp.where(same & (t > r), -BIG, 0.0)

    def score(j):
        q = q_ref[j * pair : (j + 1) * pair].reshape(rows, WIDE)
        s = lax.dot_general(q, keys[...], (((1,), (1,)), ((), ())), preferred_element_type=F32)
        if first:
            head = (s[:, :256].reshape(pair, ROWS, 256) + mask[...]).reshape(rows, 256)
            s = jnp.concatenate([head, s[:, 256:]], axis=1)
        return s

    def finish(j, s):
        peak = jnp.max(s, axis=1, keepdims=True)
        here = slice(j * pair, (j + 1) * pair)
        if not first:
            old_peak = stat_in[here, :, 0:1].reshape(rows, 1)
            old_total = stat_in[here, :, 1:2].reshape(rows, 1)
            peak = jnp.maximum(peak, old_peak)
            shrink = jnp.exp2((old_peak - peak) * SCALE2)
        weights = jnp.exp2(s * SCALE2 - peak * SCALE2)
        total = jnp.sum(weights, axis=1, keepdims=True)
        acc = jnp.dot(weights.astype(BF16), keys[:, :KVR], preferred_element_type=F32)
        if not first:
            total = total + old_total * shrink
            acc = acc + acc_in[here].reshape(rows, KVR) * shrink
        if last:
            latent = (acc * (1.0 / total)).astype(BF16)
            for k in range(pair):
                h = j * pair + k
                out_ref[:, h * VD : (h + 1) * VD] = jnp.dot(
                    latent[k * ROWS : (k + 1) * ROWS], up_ref[h], preferred_element_type=F32
                ).astype(BF16)
        else:
            lane = lax.broadcasted_iota(jnp.int32, (rows, 128), 1)
            stat_out[here] = jnp.where(lane == 0, peak, total).reshape(pair, ROWS, 128)
            acc_out[here] = acc.reshape(pair, ROWS, KVR)

    steps = group // pair
    s = score(0)
    for j in range(steps):
        after = score(j + 1) if j + 1 < steps else None
        finish(j, s)
        s = after


def attend(q, pieces, state=None, up=None, group=4):
    count = len(pieces)
    first, last = state is None, up is not None
    span = count * ROWS
    heads = lambda width: pl.BlockSpec((group, ROWS, width), lambda i: (i, 0, 0))
    in_specs = [heads(WIDE)] + [pl.BlockSpec((ROWS, WIDE), lambda i: (0, 0))] * count
    args = [q, *pieces]
    if not first:
        in_specs += [heads(128), heads(KVR)]
        args += list(state)
    if last:
        in_specs.append(pl.BlockSpec((group, KVR, VD), lambda i: (i, 0, 0)))
        args.append(up)
        out_specs = pl.BlockSpec((ROWS, group * VD), lambda i: (0, i))
        out_shape = jax.ShapeDtypeStruct((ROWS, HEADS * VD), BF16)
    else:
        out_specs = [heads(128), heads(KVR)]
        out_shape = [
            jax.ShapeDtypeStruct((HEADS, ROWS, 128), F32),
            jax.ShapeDtypeStruct((HEADS, ROWS, KVR), F32),
        ]
    scratch = [pltpu.VMEM((span, WIDE), BF16)]
    if first:
        scratch.append(pltpu.VMEM((ROWS, 256), F32))
    flops = 2 * HEADS * ROWS * span * (768 + KVR)
    return pl.pallas_call(
        functools.partial(attend_kernel, count, group, first, last),
        grid=(HEADS // group,),
        in_specs=in_specs,
        out_specs=out_specs,
        out_shape=out_shape,
        scratch_shapes=scratch,
        compiler_params=pltpu.CompilerParams(vmem_limit_bytes=VMEM_LIMIT),
        cost_estimate=pl.CostEstimate(
            flops=flops, bytes_accessed=int(16e6), transcendentals=HEADS * ROWS * span
        ),
        name="attend_first" if first else "attend_last" if last else "attend_next",
    )(*args)


def select_kernel(info, owners, pages, meta, *outs):
    depth, lo = info[0], info[1]
    row = lax.broadcasted_iota(jnp.int32, (32, 128), 0)
    lane = lax.broadcasted_iota(jnp.int32, (32, 128), 1)
    chosen = jnp.zeros((32, 128), F32)
    for p in range(PAGES):
        owner = owners[p]
        rank = jnp.int32(0)
        for earlier in range(p):
            rank = rank + jnp.where(owners[earlier] == owner, 1, 0)
        away = (owner // 2 - depth + 4) % 4
        other = (owner % 2 + lo) % 2
        slot = away * 8 + other * CAP + rank
        chosen = jnp.where((row == slot) & (lane == p), 1.0, chosen)
    chosen = chosen[:, :PAGES].astype(BF16)
    got = jnp.dot(chosen, pages[...], preferred_element_type=F32)
    tail = jnp.dot(chosen, meta[...], preferred_element_type=F32)
    for away in range(4):
        outs[away][:, :FLAT] = got[away * 8 : away * 8 + 6].astype(BF16)
        outs[away][:, FLAT:] = tail[away * 8 : away * 8 + 6].astype(BF16)


def select_pages(info, owners, pages, meta):
    smem = pl.BlockSpec(memory_space=pltpu.SMEM)
    vmem = pl.BlockSpec(memory_space=pltpu.VMEM)
    return pl.pallas_call(
        select_kernel,
        in_specs=[smem, smem, vmem, vmem],
        out_specs=[vmem] * 4,
        out_shape=[jax.ShapeDtypeStruct((2 * CAP, META), BF16)] * 4,
        compiler_params=pltpu.CompilerParams(vmem_limit_bytes=16 * 2**20),
        cost_estimate=pl.CostEstimate(flops=10**7, bytes_accessed=10**6, transcendentals=0),
        name="select_pages",
    )(info, owners, pages, meta)


def place_kernel(info, m0, m1, m2, m3, crossed, out, start):
    depth, lo = info[0], info[1]
    sub = lax.broadcasted_iota(jnp.int32, (8, 1), 0)
    mine = [m[...].astype(F32) for m in (m0, m1, m2, m3)]
    theirs = crossed[...].astype(F32)
    lane = lax.broadcasted_iota(jnp.int32, (8, 128), 1)
    eye = lax.broadcasted_iota(jnp.int32, (8, 128), 0) == lane
    place = jnp.where(lane < BLOCKS, lane * HALF, (lane - BLOCKS) * PAGE).astype(F32)
    for k in range(CAP):
        total = jnp.zeros((8, META), F32)
        for away in range(4):
            source = (depth - away + 4) % 4
            same = source * 2 + lo
            cross = source * 2 + 1 - lo
            total = jnp.where(sub == same, mine[away][k : k + 1], total)
            total = jnp.where(sub == cross, theirs[away * CAP + k : away * CAP + k + 1], total)
        out[k] = total[:, :FLAT].astype(BF16)
        mark = total[:, FLAT:]
        where = jnp.sum(mark * place, axis=1, keepdims=True)
        there = jnp.sum(jnp.where(lane < BLOCKS, mark, 0.0), axis=1, keepdims=True)
        where = jnp.where(there > 0.5, where, -1.0)
        start[k : k + 1, :] = jnp.sum(jnp.where(eye, where, 0.0), axis=0, keepdims=True).astype(
            jnp.int32
        )


def place_pages(info, own, crossed):
    smem = pl.BlockSpec(memory_space=pltpu.SMEM)
    vmem = pl.BlockSpec(memory_space=pltpu.VMEM)
    return pl.pallas_call(
        place_kernel,
        in_specs=[smem] + [vmem] * 5,
        out_specs=[vmem, vmem],
        out_shape=[
            jax.ShapeDtypeStruct((CAP, 8, FLAT), BF16),
            jax.ShapeDtypeStruct((CAP, 128), jnp.int32),
        ],
        compiler_params=pltpu.CompilerParams(vmem_limit_bytes=16 * 2**20),
        cost_estimate=pl.CostEstimate(flops=10**7, bytes_accessed=10**6, transcendentals=0),
        name="place_pages",
    )(info, *own, crossed)


def along_ctx(a, dx=0, dy=0, dc=0):
    pairs = []
    for i in range(16):
        x, y, c = i // 4, i // 2 % 2, i % 2
        pairs.append((i, (x + dx) % 4 * 4 + (y + dy) % 2 * 2 + (c + dc) % 2))
    return lax.ppermute(a, "ctx", pairs)


def along_prompt(a, dz=0, dl=0):
    pairs = [(i, (i // 2 + dz) % 4 * 2 + (i + dl) % 2) for i in range(8)]
    return lax.ppermute(a, "prompt", pairs)


def tie(a, *others):
    return lax.optimization_barrier((a, *others))[0]


def per_device(ql, kv, qu, ka, vu, block_order, page_owner):
    ql, kv = ql[0], kv[0]
    blk = block_order[0]
    marks = (blk[:, None] == jnp.arange(WIDE - LAT, dtype=jnp.int32)).astype(BF16)
    marks = jnp.broadcast_to(marks[:, None], (2, HALF, WIDE - LAT)).reshape(ROWS, WIDE - LAT)
    own = jnp.concatenate([kv, marks], axis=1)

    y = along_ctx(own, dy=1)
    xp = along_ctx(own, dx=1)
    xm = along_ctx(own, dx=3)
    own_s = along_ctx(own, dc=1)

    q = queries(block_order, tie(ql, own), qu, ka)

    prompt = lax.axis_index("prompt")
    info = jnp.stack([prompt // 2, prompt % 2]).astype(jnp.int32)
    pages = kv.reshape(PAGES, FLAT)
    page = jnp.arange(PAGES, dtype=jnp.int32)
    column = jnp.arange(128, dtype=jnp.int32)
    meta = (column == blk[page // 6][:, None]) | (column == BLOCKS + page[:, None] % 6)
    cut = select_pages(info, page_owner[0, :, 0], pages, meta.astype(BF16))
    own_cut = [cut[0]] + [along_prompt(cut[dz], dz=dz) for dz in (1, 2, 3)]
    crossed = along_prompt(jnp.concatenate([c[CAP:] for c in own_cut], axis=0), dl=1)

    yxp = along_ctx(y, dx=1)
    yxm = along_ctx(y, dx=3)
    x2 = along_ctx(own, dx=2)
    yx2 = along_ctx(y, dx=2)
    near = [own, y, xp, xm]
    near_s = [own_s] + [along_ctx(a, dc=1) for a in near[1:]]
    state = attend(q, near + near_s)
    far = [yxp, yxm, x2, yx2]
    far_s = [along_ctx(a, dc=1) for a in far]
    out = attend(q, far + far_s, state, vu)

    cache, start = place_pages(info, own_cut, crossed)
    cache = jnp.transpose(cache, (1, 0, 2))[None, None]
    start = jnp.transpose(start[:, :8], (1, 0))[None, None]
    return out[None], cache, start


def solution(mesh):
    return jax.shard_map(
        per_device,
        mesh=mesh,
        in_specs=(
            P("prompt", "ctx", None),
            P("prompt", "ctx", None),
            P(),
            P(),
            P(),
            P("prompt", "ctx"),
            P("prompt", "ctx", None),
        ),
        out_specs=(
            P("prompt", "ctx", None),
            P("prompt", "ctx", None, None, None),
            P("prompt", "ctx", None, None),
        ),
        check_vma=False,
    )
```

```python
import functools
import math

import jax
import jax.numpy as jnp
import numpy as np
from jax import lax
from jax.experimental import pallas as pl
from jax.experimental.pallas import tpu as pltpu
from jax.sharding import PartitionSpec as P

F32 = jnp.float32
BF16 = jnp.bfloat16
NOPE, ROPE, KVR, VD, HEADS = 128, 64, 512, 128, 16
LAT = KVR + ROPE
WIDE = 640
PAGE, PAGES, CAP = 16, 12, 3
HALF, ROWS = 96, 192
BLOCKS = 32
FLAT = PAGE * LAT
BIG = 1e30
SCALE2 = (NOPE + ROPE) ** -0.5 * math.log2(math.e)
VMEM_LIMIT = 60 * 2**20
ATTEND_VMEM = 52 * 2**20
SMALL_VMEM = 8 * 2**20


def rope_tables():
    lane = np.arange(128)
    freq = 10000.0 ** (-2.0 * (lane % 32) / ROPE)
    sign = np.where(lane % 64 < 32, -1.0, 1.0)

    def table(places):
        angle = places[:, None] * freq
        return np.concatenate([np.cos(angle), sign * np.sin(angle)], axis=1).astype(np.float32)

    return table(np.arange(BLOCKS) * float(HALF)), table(np.arange(HALF) * 1.0)


def query_kernel(
    blk_h, ql_h, qu_h, ka_h, tab_h, _, out_h, token, blk, ql, qu, ka, tab, out, rope_s, ext_s, sem
):
    chunks = qu.shape[0]
    width = qu.shape[2]
    copies = [
        pltpu.make_async_copy(blk_h, blk, sem.at[0]),
        pltpu.make_async_copy(tab_h, tab, sem.at[1]),
        pltpu.make_async_copy(ql_h, ql, sem.at[2]),
    ]
    for j in range(chunks):
        part = qu_h.at[:, j * width : (j + 1) * width]
        copies.append(pltpu.make_async_copy(part, qu.at[j], sem.at[4 + j]))
    copies.insert(4, pltpu.make_async_copy(ka_h, ka, sem.at[3]))
    for copy in copies:
        copy.start()
    copies[0].wait()
    copies[1].wait()
    half_lane = lax.broadcasted_iota(jnp.int32, (HALF, 128), 1)
    for slot in range(2):
        here = blk[0, slot]
        base = tab[pl.ds(here, 1), :]
        bc, bs = base[:, :128], base[:, 128:]
        oc, os = tab[BLOCKS:, :128], tab[BLOCKS:, 128:]
        rows = slice(slot * HALF, (slot + 1) * HALF)
        rope_s[rows, :128] = bc * oc - bs * os
        rope_s[rows, 128:] = bs * oc + bc * os
        later = (half_lane >= 64 + here + 1) & (half_lane < 64 + BLOCKS)
        ext_s[rows, :] = jnp.where(later, -BIG, 0.0)
    lane = lax.broadcasted_iota(jnp.int32, (ROWS, 128), 1)
    low = lane < 64
    token[...] = jnp.zeros(token.shape, F32)
    copies[2].wait()
    outgoing = []
    for c in range(chunks):
        copies[3 if c == 0 else 4 + c].wait()
        both = jnp.dot(ql[...], qu[c], preferred_element_type=F32).astype(BF16)
        if c == 0:
            copies[4].wait()
        for j in range(width // 384):
            even, at = (c * width // 384 + j) * 2, 384 * j
            t0 = both[:, at : at + 128]
            t1 = both[:, at + 128 : at + 256].astype(F32)
            t2 = both[:, at + 256 : at + 384].astype(F32)
            odd = jnp.where(low, t2, t1).astype(BF16)
            pair = jnp.where(low, t1, t2)
            swapped = jnp.where(lane % 64 < 32, pltpu.roll(pair, 96, 1), pltpu.roll(pair, 32, 1))
            turned = pair * rope_s[:, :128] + swapped * rope_s[:, 128:]
            out[even, :, :KVR] = jnp.dot(t0, ka[even], preferred_element_type=F32).astype(BF16)
            odd_key = jnp.concatenate([ka[even + 1, 64:, :], ka[even + 1, :64, :]], axis=0)
            out[even + 1, :, :KVR] = jnp.dot(odd, odd_key, preferred_element_type=F32).astype(BF16)
            out[even, :, KVR:] = jnp.where(low, turned, ext_s[...]).astype(BF16)
            turned = pltpu.roll(turned, 64, 1)
            out[even + 1, :, KVR:] = jnp.where(low, turned, ext_s[...]).astype(BF16)
        heads = pl.ds(c * HEADS // chunks, HEADS // chunks)
        done = pltpu.make_async_copy(out.at[heads], out_h.at[heads], sem.at[4 + chunks + c])
        done.start()
        outgoing.append(done)
    for done in outgoing:
        done.wait()


HBM = pl.BlockSpec(memory_space=pltpu.HBM)
VMEM = pl.BlockSpec(memory_space=pltpu.VMEM)
TOKEN = jax.ShapeDtypeStruct((8, 128), F32)


def queries(blk, ql, qu, ka, follow, chunks=4):
    width = qu.shape[1] // chunks
    table = np.concatenate(rope_tables(), axis=0)
    return pl.pallas_call(
        query_kernel,
        in_specs=[HBM] * 6,
        out_specs=[HBM, VMEM],
        scratch_shapes=[
            pltpu.SMEM(blk.shape, jnp.int32),
            pltpu.VMEM(ql.shape, BF16),
            pltpu.VMEM((chunks, qu.shape[0], width), BF16),
            pltpu.VMEM(ka.shape, BF16),
            pltpu.VMEM(table.shape, F32),
            pltpu.VMEM((HEADS, ROWS, WIDE), BF16),
            pltpu.VMEM((ROWS, 256), F32),
            pltpu.VMEM((ROWS, 128), F32),
            pltpu.SemaphoreType.DMA((4 + 2 * chunks,)),
        ],
        out_shape=[jax.ShapeDtypeStruct((HEADS, ROWS, WIDE), BF16), TOKEN],
        compiler_params=pltpu.CompilerParams(vmem_limit_bytes=VMEM_LIMIT),
        cost_estimate=pl.CostEstimate(
            flops=int(2.6e9), bytes_accessed=int(15e6), transcendentals=0
        ),
        name="queries",
    )(blk, ql, qu, ka, jnp.asarray(table), follow)


def join_kernel(count, *refs):
    out = refs[-1]
    at = 0
    for piece in refs[:count]:
        out[at : at + piece.shape[0], :] = piece[...]
        at += piece.shape[0]


def join(pieces, follow=None, limit=None):
    rows = sum(piece.shape[0] for piece in pieces)
    follow = [] if follow is None else [follow]
    return pl.pallas_call(
        functools.partial(join_kernel, len(pieces)),
        in_specs=[VMEM] * len(pieces) + [HBM] * len(follow),
        out_specs=VMEM,
        out_shape=jax.ShapeDtypeStruct((rows, WIDE), BF16),
        compiler_params=pltpu.CompilerParams(vmem_limit_bytes=limit or SMALL_VMEM),
        cost_estimate=pl.CostEstimate(flops=0, bytes_accessed=10**6, transcendentals=0),
        name="join",
    )(*pieces, *follow)


def attend_kernel(sizes, group, first, last, follows, *refs):
    refs = list(refs)
    q_ref = refs.pop(0)
    pieces = [refs.pop(0) for _ in sizes]
    if follows:
        refs.pop(0)
    if not first:
        state_in = refs.pop(0)
    if last:
        up_ref, out_ref = refs.pop(0), refs.pop(0)
    else:
        state_out, token = refs.pop(0), refs.pop(0)
    keys = refs.pop(0)
    mask = refs.pop(0) if first else None
    pair = 2
    rows = pair * ROWS

    @pl.when(pl.program_id(0) == 0)
    def _():
        at = 0
        for size, piece in zip(sizes, pieces):
            keys[at : at + size, :] = piece[...]
            at += size
        if not last:
            token[...] = jnp.zeros(token.shape, F32)
        if first:
            r = lax.broadcasted_iota(jnp.int32, (ROWS, 256), 0)
            t = lax.broadcasted_iota(jnp.int32, (ROWS, 256), 1)
            same = ((r < HALF) & (t < HALF)) | ((r >= HALF) & (t >= HALF) & (t < ROWS))
            mask[...] = jnp.where(same & (t > r), -BIG, 0.0)

    def score(j):
        q = q_ref[j * pair : (j + 1) * pair].reshape(rows, WIDE)
        s = lax.dot_general(q, keys[...], (((1,), (1,)), ((), ())), preferred_element_type=F32)
        if first:
            head = (s[:, :256].reshape(pair, ROWS, 256) + mask[...]).reshape(rows, 256)
            s = jnp.concatenate([head, s[:, 256:]], axis=1)
        return s

    def finish(j, s):
        peak = jnp.max(s, axis=1, keepdims=True)
        here = slice(j * pair, (j + 1) * pair)
        if not first:
            marks = state_in[here, :, KVR:].reshape(rows, 128).astype(F32)
            old_peak = marks[:, 0:1] + marks[:, 1:2] + marks[:, 2:3]
            old_total = marks[:, 3:4] + marks[:, 4:5] + marks[:, 5:6]
            peak = jnp.maximum(peak, old_peak)
            shrink = jnp.exp2((old_peak - peak) * SCALE2)
        weights = jnp.exp2(s * SCALE2 - peak * SCALE2)
        total = jnp.sum(weights, axis=1, keepdims=True)
        acc = jnp.dot(weights.astype(BF16), keys[:, :KVR], preferred_element_type=F32)
        if not first:
            total = total + old_total * shrink
            acc = acc + state_in[here, :, :KVR].reshape(rows, KVR).astype(F32) * shrink
        if last:
            latent = (acc * (1.0 / total)).astype(BF16)
            for k in range(pair):
                h = j * pair + k
                out_ref[:, h * VD : (h + 1) * VD] = jnp.dot(
                    latent[k * ROWS : (k + 1) * ROWS], up_ref[h], preferred_element_type=F32
                ).astype(BF16)
        else:
            lane = lax.broadcasted_iota(jnp.int32, (rows, 128), 1)
            marks = jnp.zeros((rows, 128), F32)
            for base, rest in ((0, peak), (3, total)):
                for part in range(3):
                    top = rest.astype(BF16).astype(F32)
                    marks = jnp.where(lane == base + part, top, marks)
                    rest = rest - top
            state_out[here, :, KVR:] = marks.astype(BF16).reshape(pair, ROWS, 128)
            state_out[here, :, :KVR] = acc.astype(BF16).reshape(pair, ROWS, KVR)

    steps = group // pair
    s = score(0)
    for j in range(steps):
        after = score(j + 1) if j + 1 < steps else None
        finish(j, s)
        s = after


def attend(q, pieces, state=None, up=None, group=4, follow=None):
    sizes = [piece.shape[0] for piece in pieces]
    first, last = state is None, up is not None
    span = sum(sizes)
    heads = lambda width: pl.BlockSpec((group, ROWS, width), lambda i: (i, 0, 0))
    in_specs = [heads(WIDE)] + [pl.BlockSpec((n, WIDE), lambda i: (0, 0)) for n in sizes]
    args = [q, *pieces]
    if follow is not None:
        in_specs.append(HBM)
        args.append(follow)
    if not first:
        in_specs.append(heads(WIDE))
        args.append(state)
    if last:
        in_specs.append(pl.BlockSpec((group, KVR, VD), lambda i: (i, 0, 0)))
        args.append(up)
        out_specs = pl.BlockSpec((ROWS, group * VD), lambda i: (0, i))
        out_shape = jax.ShapeDtypeStruct((ROWS, HEADS * VD), BF16)
    else:
        out_specs = [heads(WIDE), pl.BlockSpec((8, 128), lambda i: (0, 0))]
        out_shape = [
            jax.ShapeDtypeStruct((HEADS, ROWS, WIDE), BF16),
            TOKEN,
        ]
    scratch = [pltpu.VMEM((span, WIDE), BF16)]
    if first:
        scratch.append(pltpu.VMEM((ROWS, 256), F32))
    flops = 2 * HEADS * ROWS * span * (768 + KVR)
    return pl.pallas_call(
        functools.partial(attend_kernel, sizes, group, first, last, follow is not None),
        grid=(HEADS // group,),
        in_specs=in_specs,
        out_specs=out_specs,
        out_shape=out_shape,
        scratch_shapes=scratch,
        compiler_params=pltpu.CompilerParams(vmem_limit_bytes=ATTEND_VMEM),
        cost_estimate=pl.CostEstimate(
            flops=flops, bytes_accessed=int(16e6), transcendentals=HEADS * ROWS * span
        ),
        name="attend_first" if first else "attend_last" if last else "attend_next",
    )(*args)


def pack_kernel(blk_h, owners_h, kv_h, out, cut, blk, owners, kv, sem):
    copies = [
        pltpu.make_async_copy(blk_h, blk, sem.at[0]),
        pltpu.make_async_copy(owners_h, owners, sem.at[1]),
        pltpu.make_async_copy(kv_h, kv, sem.at[2]),
    ]
    for copy in copies:
        copy.start()
    cut[...] = jnp.zeros(cut.shape, BF16)
    row = lax.broadcasted_iota(jnp.int32, (ROWS, 128), 0)
    lane = lax.broadcasted_iota(jnp.int32, (ROWS, 128), 1)
    copies[0].wait()
    copies[1].wait()
    first = row < HALF
    marks = (lane == 64 + jnp.where(first, blk[0, 0], blk[0, 1])) | (
        lane == 64 + BLOCKS + jnp.where(first, row, row - HALF) // PAGE
    )
    copies[2].wait()
    out[:, :KVR] = kv[:, :KVR]
    tail = jnp.concatenate([kv[:, KVR:], jnp.zeros((ROWS, 64), BF16)], axis=1).astype(F32)
    out[:, KVR:] = jnp.where(marks, 1.0, tail).astype(BF16)
    for p in range(PAGES):
        owner = owners[0, p]
        rank = jnp.int32(0)
        for earlier in range(p):
            rank = rank + jnp.where(owners[0, earlier] == owner, 1, 0)
        at = pl.multiple_of((owner * CAP + rank) * PAGE, PAGE)
        cut[pl.ds(at, PAGE), :] = out[p * PAGE : (p + 1) * PAGE, :]


def pack(blk, owners, kv):
    return pl.pallas_call(
        pack_kernel,
        in_specs=[HBM, HBM, HBM],
        out_specs=[VMEM, VMEM],
        out_shape=[
            jax.ShapeDtypeStruct((ROWS, WIDE), BF16),
            jax.ShapeDtypeStruct((8 * CAP * PAGE, WIDE), BF16),
        ],
        scratch_shapes=[
            pltpu.SMEM(blk.shape, jnp.int32),
            pltpu.SMEM(owners.shape, jnp.int32),
            pltpu.VMEM(kv.shape, BF16),
            pltpu.SemaphoreType.DMA((3,)),
        ],
        compiler_params=pltpu.CompilerParams(vmem_limit_bytes=VMEM_LIMIT),
        cost_estimate=pl.CostEstimate(flops=10**5, bytes_accessed=10**6, transcendentals=0),
        name="pack",
    )(blk, owners, kv)


def place_kernel(got, _, out, start, wide):
    rows = CAP * PAGE
    for t in range(WIDE // 128):
        wide[t] = got[:, t * 128 : (t + 1) * 128].astype(F32)
    lane = lax.broadcasted_iota(jnp.int32, (8, 128), 1)
    eye = lax.broadcasted_iota(jnp.int32, (8, 128), 0) == lane
    is_block = (lane >= 64) & (lane < 64 + BLOCKS)
    is_page = (lane >= 64 + BLOCKS) & (lane < 70 + BLOCKS)
    place = jnp.where(is_block, (lane - 64) * HALF, (lane - 64 - BLOCKS) * PAGE).astype(F32)
    place = jnp.where(is_block | is_page, place, 0.0)
    for k in range(CAP):
        for r in range(0, PAGE, 2):
            pair = []
            for i in range(2):
                every = pl.ds(k * PAGE + r + i, 8, stride=rows)
                parts = [wide[t, every, :] for t in range(WIDE // 128)]
                pair.append(jnp.concatenate(parts, axis=1))
            if r == 0:
                mark = pair[0][:, KVR:]
                where = jnp.sum(mark * place, axis=1, keepdims=True)
                there = jnp.sum(jnp.where(is_block, mark, 0.0), axis=1, keepdims=True)
                where = jnp.where(there > 0.5, where, -1.0)
                where = jnp.sum(jnp.where(eye, where, 0.0), axis=0, keepdims=True)
                start[k] = where[:, :8].astype(jnp.int32)
            both = jnp.concatenate([pair[0][:, :LAT], pair[1][:, :LAT]], axis=1)
            out[k, :, r * LAT : (r + 2) * LAT] = both.astype(BF16)


def place_pages(got, follow):
    return pl.pallas_call(
        place_kernel,
        in_specs=[VMEM, HBM],
        out_specs=[VMEM, VMEM],
        out_shape=[
            jax.ShapeDtypeStruct((CAP, 8, FLAT), BF16),
            jax.ShapeDtypeStruct((CAP, 1, 8), jnp.int32),
        ],
        scratch_shapes=[pltpu.VMEM((WIDE // 128, got.shape[0], 128), F32)],
        compiler_params=pltpu.CompilerParams(vmem_limit_bytes=SMALL_VMEM),
        cost_estimate=pl.CostEstimate(flops=10**7, bytes_accessed=10**6, transcendentals=0),
        name="place_pages",
    )(got, follow)


def along_ctx(a, dx=0, dy=0, dc=0):
    pairs = []
    for i in range(16):
        x, y, c = i // 4, i // 2 % 2, i % 2
        pairs.append((i, (x + dx) % 4 * 4 + (y + dy) % 2 * 2 + (c + dc) % 2))
    return lax.ppermute(a, "ctx", pairs)


def per_device(ql, kv, qu, ka, vu, block_order, page_owner):
    ql, kv = ql[0], kv[0]
    own, cut = pack(block_order, page_owner[:, :, 0], kv)
    y = along_ctx(own, dy=1)
    xp = along_ctx(own, dx=1)
    xm = along_ctx(own, dx=3)
    x2 = along_ctx(own, dx=2)
    got = lax.all_to_all(cut.reshape(8, CAP * PAGE, WIDE), "prompt", 0, 0, tiled=True)
    got = got.reshape(8 * CAP * PAGE, WIDE)
    q, token = queries(block_order, ql, qu, ka, own)
    y = join([y], token)
    yxp = along_ctx(y, dx=1)
    yxm = along_ctx(y, dx=3)
    yx2 = along_ctx(y, dx=2)
    near = [own, y, xp, xm]
    near += [along_ctx(a, dc=1) for a in near]
    state, token = attend(q, near)
    cache, start = place_pages(got, token)
    far = join([x2, yxp, yxm, yx2], start)
    far_s = along_ctx(far, dc=1)
    out = attend(q, [far, far_s], state, vu)

    cache = jnp.transpose(cache, (1, 0, 2))[None, None]
    start = jnp.transpose(start, (1, 2, 0))[None]
    return out[None], cache, start


def solution(mesh):
    return jax.shard_map(
        per_device,
        mesh=mesh,
        in_specs=(
            P("prompt", "ctx", None),
            P("prompt", "ctx", None),
            P(),
            P(),
            P(),
            P("prompt", "ctx"),
            P("prompt", "ctx", None),
        ),
        out_specs=(
            P("prompt", "ctx", None),
            P("prompt", "ctx", None, None, None),
            P("prompt", "ctx", None, None),
        ),
        check_vma=False,
    )
```

```python
import functools
import math

import jax
import jax.numpy as jnp
import numpy as np
from jax import lax
from jax.experimental import pallas as pl
from jax.experimental.pallas import tpu as pltpu
from jax.sharding import PartitionSpec as P

F32 = jnp.float32
BF16 = jnp.bfloat16
NOPE, ROPE, KVR, VD, HEADS = 128, 64, 512, 128, 16
LAT = KVR + ROPE
WIDE = 640
PAGE, PAGES, CAP = 16, 12, 3
HALF, ROWS = 96, 192
BLOCKS = 32
FLAT = PAGE * LAT
BIG = 1e30
SCALE2 = (NOPE + ROPE) ** -0.5 * math.log2(math.e)
VMEM_LIMIT = 60 * 2**20
QUERY_VMEM = 60 * 2**20
ATTEND_VMEM = 52 * 2**20
SMALL_VMEM = 8 * 2**20


def rope_tables():
    lane = np.arange(128)
    freq = 10000.0 ** (-2.0 * (lane % 32) / ROPE)
    sign = np.where(lane % 64 < 32, -1.0, 1.0)

    def table(places):
        angle = places[:, None] * freq
        return np.concatenate([np.cos(angle), sign * np.sin(angle)], axis=1).astype(np.float32)

    return table(np.arange(BLOCKS) * float(HALF)), table(np.arange(HALF) * 1.0)


def query_kernel(
    blk_h, ql_h, qu_h, ka_h, tab_h, _, out_h, token, blk, ql, qu, ka, tab, out, rope_s, ext_s, sem
):
    chunks = qu.shape[0]
    width = qu.shape[2]
    copies = [
        pltpu.make_async_copy(blk_h, blk, sem.at[0]),
        pltpu.make_async_copy(tab_h, tab, sem.at[1]),
        pltpu.make_async_copy(ql_h, ql, sem.at[2]),
    ]
    for j in range(chunks):
        part = qu_h.at[:, j * width : (j + 1) * width]
        copies.append(pltpu.make_async_copy(part, qu.at[j], sem.at[4 + j]))
    copies.insert(4, pltpu.make_async_copy(ka_h, ka, sem.at[3]))
    for copy in copies:
        copy.start()
    copies[0].wait()
    copies[1].wait()
    half_lane = lax.broadcasted_iota(jnp.int32, (HALF, 128), 1)
    for slot in range(2):
        here = blk[0, slot]
        base = tab[pl.ds(here, 1), :]
        bc, bs = base[:, :128], base[:, 128:]
        oc, os = tab[BLOCKS:, :128], tab[BLOCKS:, 128:]
        rows = slice(slot * HALF, (slot + 1) * HALF)
        rope_s[rows, :128] = bc * oc - bs * os
        rope_s[rows, 128:] = bs * oc + bc * os
        later = (half_lane >= 64 + here + 1) & (half_lane < 64 + BLOCKS)
        ext_s[rows, :] = jnp.where(later, -BIG, 0.0)
    lane = lax.broadcasted_iota(jnp.int32, (ROWS, 128), 1)
    low = lane < 64
    token[...] = jnp.zeros(token.shape, F32)
    copies[2].wait()
    outgoing = []
    for c in range(chunks):
        copies[3 if c == 0 else 4 + c].wait()
        both = jnp.dot(ql[...], qu[c], preferred_element_type=F32).astype(BF16)
        if c == 0:
            copies[4].wait()
        for j in range(width // 384):
            even, at = (c * width // 384 + j) * 2, 384 * j
            t0 = both[:, at : at + 128]
            t1 = both[:, at + 128 : at + 256].astype(F32)
            t2 = both[:, at + 256 : at + 384].astype(F32)
            odd = jnp.where(low, t2, t1).astype(BF16)
            pair = jnp.where(low, t1, t2)
            swapped = jnp.where(lane % 64 < 32, pltpu.roll(pair, 96, 1), pltpu.roll(pair, 32, 1))
            turned = pair * rope_s[:, :128] + swapped * rope_s[:, 128:]
            out[even, :, :KVR] = jnp.dot(t0, ka[even], preferred_element_type=F32).astype(BF16)
            odd_key = jnp.concatenate([ka[even + 1, 64:, :], ka[even + 1, :64, :]], axis=0)
            out[even + 1, :, :KVR] = jnp.dot(odd, odd_key, preferred_element_type=F32).astype(BF16)
            out[even, :, KVR:] = jnp.where(low, turned, ext_s[...]).astype(BF16)
            turned = pltpu.roll(turned, 64, 1)
            out[even + 1, :, KVR:] = jnp.where(low, turned, ext_s[...]).astype(BF16)
        heads = pl.ds(c * HEADS // chunks, HEADS // chunks)
        done = pltpu.make_async_copy(out.at[heads], out_h.at[heads], sem.at[4 + chunks + c])
        done.start()
        outgoing.append(done)
    for done in outgoing:
        done.wait()


HBM = pl.BlockSpec(memory_space=pltpu.HBM)
VMEM = pl.BlockSpec(memory_space=pltpu.VMEM)
TOKEN = jax.ShapeDtypeStruct((8, 128), F32)


def queries(blk, ql, qu, ka, follow, chunks=4):
    width = qu.shape[1] // chunks
    table = np.concatenate(rope_tables(), axis=0)
    return pl.pallas_call(
        query_kernel,
        in_specs=[HBM] * 6,
        out_specs=[HBM, VMEM],
        scratch_shapes=[
            pltpu.SMEM(blk.shape, jnp.int32),
            pltpu.VMEM(ql.shape, BF16),
            pltpu.VMEM((chunks, qu.shape[0], width), BF16),
            pltpu.VMEM(ka.shape, BF16),
            pltpu.VMEM(table.shape, F32),
            pltpu.VMEM((HEADS, ROWS, WIDE), BF16),
            pltpu.VMEM((ROWS, 256), F32),
            pltpu.VMEM((ROWS, 128), F32),
            pltpu.SemaphoreType.DMA((4 + 2 * chunks,)),
        ],
        out_shape=[jax.ShapeDtypeStruct((HEADS, ROWS, WIDE), BF16), TOKEN],
        compiler_params=pltpu.CompilerParams(vmem_limit_bytes=QUERY_VMEM),
        cost_estimate=pl.CostEstimate(
            flops=int(2.6e9), bytes_accessed=int(15e6), transcendentals=0
        ),
        name="queries",
    )(blk, ql, qu, ka, jnp.asarray(table), follow)


def join_kernel(count, groups, *refs):
    outs = refs[len(refs) - len(groups) :]
    for group, out in zip(groups, outs):
        at = 0
        for i in group:
            piece = refs[i]
            out[at : at + piece.shape[0], :] = piece[...]
            at += piece.shape[0]


def join(pieces, groups, *follow):
    rows = [sum(pieces[i].shape[0] for i in group) for group in groups]
    return pl.pallas_call(
        functools.partial(join_kernel, len(pieces), groups),
        in_specs=[VMEM] * len(pieces) + [HBM] * len(follow),
        out_specs=[VMEM] * len(groups),
        out_shape=[jax.ShapeDtypeStruct((n, WIDE), BF16) for n in rows],
        compiler_params=pltpu.CompilerParams(vmem_limit_bytes=SMALL_VMEM),
        cost_estimate=pl.CostEstimate(flops=0, bytes_accessed=10**6, transcendentals=0),
        name="join",
    )(*pieces, *follow)


def attend_kernel(sizes, group, first, last, follows, *refs):
    refs = list(refs)
    q_ref = refs.pop(0)
    pieces = [refs.pop(0) for _ in sizes]
    if follows:
        refs.pop(0)
    if not first:
        state_in = refs.pop(0)
    if last:
        up_ref, out_ref = refs.pop(0), refs.pop(0)
    else:
        state_out, token = refs.pop(0), refs.pop(0)
    keys = refs.pop(0)
    mask = refs.pop(0) if first else None
    pair = 2
    rows = pair * ROWS

    @pl.when(pl.program_id(0) == 0)
    def _():
        at = 0
        for size, piece in zip(sizes, pieces):
            keys[at : at + size, :] = piece[...]
            at += size
        if not last:
            token[...] = jnp.zeros(token.shape, F32)
        if first:
            r = lax.broadcasted_iota(jnp.int32, (ROWS, 256), 0)
            t = lax.broadcasted_iota(jnp.int32, (ROWS, 256), 1)
            same = ((r < HALF) & (t < HALF)) | ((r >= HALF) & (t >= HALF) & (t < ROWS))
            mask[...] = jnp.where(same & (t > r), -BIG, 0.0)

    def score(j):
        q = q_ref[j * pair : (j + 1) * pair].reshape(rows, WIDE)
        s = lax.dot_general(q, keys[...], (((1,), (1,)), ((), ())), preferred_element_type=F32)
        if first:
            head = (s[:, :256].reshape(pair, ROWS, 256) + mask[...]).reshape(rows, 256)
            s = jnp.concatenate([head, s[:, 256:]], axis=1)
        return s

    def finish(j, s):
        peak = jnp.max(s, axis=1, keepdims=True)
        here = slice(j * pair, (j + 1) * pair)
        if not first:
            marks = state_in[here, :, KVR:].reshape(rows, 128).astype(F32)
            old_peak = marks[:, 0:1] + marks[:, 1:2] + marks[:, 2:3]
            old_total = marks[:, 3:4] + marks[:, 4:5] + marks[:, 5:6]
            peak = jnp.maximum(peak, old_peak)
            shrink = jnp.exp2((old_peak - peak) * SCALE2)
        weights = jnp.exp2(s * SCALE2 - peak * SCALE2)
        total = jnp.sum(weights, axis=1, keepdims=True)
        acc = jnp.dot(weights.astype(BF16), keys[:, :KVR], preferred_element_type=F32)
        if not first:
            total = total + old_total * shrink
            acc = acc + state_in[here, :, :KVR].reshape(rows, KVR).astype(F32) * shrink
        if last:
            latent = (acc * (1.0 / total)).astype(BF16)
            for k in range(pair):
                h = j * pair + k
                out_ref[:, h * VD : (h + 1) * VD] = jnp.dot(
                    latent[k * ROWS : (k + 1) * ROWS], up_ref[h], preferred_element_type=F32
                ).astype(BF16)
        else:
            lane = lax.broadcasted_iota(jnp.int32, (rows, 128), 1)
            marks = jnp.zeros((rows, 128), F32)
            for base, rest in ((0, peak), (3, total)):
                for part in range(3):
                    top = rest.astype(BF16).astype(F32)
                    marks = jnp.where(lane == base + part, top, marks)
                    rest = rest - top
            state_out[here, :, KVR:] = marks.astype(BF16).reshape(pair, ROWS, 128)
            state_out[here, :, :KVR] = acc.astype(BF16).reshape(pair, ROWS, KVR)

    steps = group // pair
    s = score(0)
    for j in range(steps):
        after = score(j + 1) if j + 1 < steps else None
        finish(j, s)
        s = after


def attend(q, pieces, state=None, up=None, group=4, follow=None):
    pieces = [piece if isinstance(piece, tuple) else (piece, 0, piece.shape[0]) for piece in pieces]
    sizes = [size for _, _, size in pieces]
    first, last = state is None, up is not None
    span = sum(sizes)
    heads = lambda width: pl.BlockSpec((group, ROWS, width), lambda i: (i, 0, 0))
    in_specs = [heads(WIDE)] + [
        pl.BlockSpec((size, WIDE), lambda i, at=at: (at, 0)) for _, at, size in pieces
    ]
    args = [q, *(piece for piece, _, _ in pieces)]
    if follow is not None:
        in_specs.append(HBM)
        args.append(follow)
    if not first:
        in_specs.append(heads(WIDE))
        args.append(state)
    if last:
        in_specs.append(pl.BlockSpec((group, KVR, VD), lambda i: (i, 0, 0)))
        args.append(up)
        out_specs = pl.BlockSpec((ROWS, group * VD), lambda i: (0, i))
        out_shape = jax.ShapeDtypeStruct((ROWS, HEADS * VD), BF16)
    else:
        out_specs = [heads(WIDE), pl.BlockSpec((8, 128), lambda i: (0, 0))]
        out_shape = [
            jax.ShapeDtypeStruct((HEADS, ROWS, WIDE), BF16),
            TOKEN,
        ]
    scratch = [pltpu.VMEM((span, WIDE), BF16)]
    if first:
        scratch.append(pltpu.VMEM((ROWS, 256), F32))
    flops = 2 * HEADS * ROWS * span * (768 + KVR)
    return pl.pallas_call(
        functools.partial(attend_kernel, sizes, group, first, last, follow is not None),
        grid=(HEADS // group,),
        in_specs=in_specs,
        out_specs=out_specs,
        out_shape=out_shape,
        scratch_shapes=scratch,
        compiler_params=pltpu.CompilerParams(vmem_limit_bytes=ATTEND_VMEM),
        cost_estimate=pl.CostEstimate(
            flops=flops, bytes_accessed=int(16e6), transcendentals=HEADS * ROWS * span
        ),
        name="attend_first" if first else "attend_last" if last else "attend_next",
    )(*args)


def pack_kernel(blk_h, owners_h, kv_h, out, cut, blk, owners, kv, sem):
    copies = [
        pltpu.make_async_copy(blk_h, blk, sem.at[0]),
        pltpu.make_async_copy(owners_h, owners, sem.at[1]),
        pltpu.make_async_copy(kv_h, kv, sem.at[2]),
    ]
    for copy in copies:
        copy.start()
    cut[...] = jnp.zeros(cut.shape, BF16)
    row = lax.broadcasted_iota(jnp.int32, (ROWS, 128), 0)
    lane = lax.broadcasted_iota(jnp.int32, (ROWS, 128), 1)
    copies[0].wait()
    copies[1].wait()
    first = row < HALF
    marks = (lane == 64 + jnp.where(first, blk[0, 0], blk[0, 1])) | (
        lane == 64 + BLOCKS + jnp.where(first, row, row - HALF) // PAGE
    )
    copies[2].wait()
    out[:, :KVR] = kv[:, :KVR]
    tail = jnp.concatenate([kv[:, KVR:], jnp.zeros((ROWS, 64), BF16)], axis=1).astype(F32)
    out[:, KVR:] = jnp.where(marks, 1.0, tail).astype(BF16)
    for p in range(PAGES):
        owner = owners[0, p]
        rank = jnp.int32(0)
        for earlier in range(p):
            rank = rank + jnp.where(owners[0, earlier] == owner, 1, 0)
        at = pl.multiple_of((owner * CAP + rank) * PAGE, PAGE)
        cut[pl.ds(at, PAGE), :] = out[p * PAGE : (p + 1) * PAGE, :]


def pack(blk, owners, kv):
    return pl.pallas_call(
        pack_kernel,
        in_specs=[HBM, HBM, HBM],
        out_specs=[VMEM, VMEM],
        out_shape=[
            jax.ShapeDtypeStruct((ROWS, WIDE), BF16),
            jax.ShapeDtypeStruct((8 * CAP * PAGE, WIDE), BF16),
        ],
        scratch_shapes=[
            pltpu.SMEM(blk.shape, jnp.int32),
            pltpu.SMEM(owners.shape, jnp.int32),
            pltpu.VMEM(kv.shape, BF16),
            pltpu.SemaphoreType.DMA((3,)),
        ],
        compiler_params=pltpu.CompilerParams(vmem_limit_bytes=VMEM_LIMIT),
        cost_estimate=pl.CostEstimate(flops=10**5, bytes_accessed=10**6, transcendentals=0),
        name="pack",
    )(blk, owners, kv)


def place_kernel(got, _, out, start, wide):
    rows = CAP * PAGE
    for t in range(WIDE // 128):
        wide[t] = got[:, t * 128 : (t + 1) * 128].astype(F32)
    lane = lax.broadcasted_iota(jnp.int32, (8, 128), 1)
    eye = lax.broadcasted_iota(jnp.int32, (8, 128), 0) == lane
    is_block = (lane >= 64) & (lane < 64 + BLOCKS)
    is_page = (lane >= 64 + BLOCKS) & (lane < 70 + BLOCKS)
    place = jnp.where(is_block, (lane - 64) * HALF, (lane - 64 - BLOCKS) * PAGE).astype(F32)
    place = jnp.where(is_block | is_page, place, 0.0)
    for k in range(CAP):
        for r in range(0, PAGE, 2):
            pair = []
            for i in range(2):
                every = pl.ds(k * PAGE + r + i, 8, stride=rows)
                parts = [wide[t, every, :] for t in range(WIDE // 128)]
                pair.append(jnp.concatenate(parts, axis=1))
            if r == 0:
                mark = pair[0][:, KVR:]
                where = jnp.sum(mark * place, axis=1, keepdims=True)
                there = jnp.sum(jnp.where(is_block, mark, 0.0), axis=1, keepdims=True)
                where = jnp.where(there > 0.5, where, -1.0)
                where = jnp.sum(jnp.where(eye, where, 0.0), axis=0, keepdims=True)
                start[k] = where[:, :8].astype(jnp.int32)
            both = jnp.concatenate([pair[0][:, :LAT], pair[1][:, :LAT]], axis=1)
            out[k, :, r * LAT : (r + 2) * LAT] = both.astype(BF16)


def place_pages(got, follow):
    return pl.pallas_call(
        place_kernel,
        in_specs=[VMEM, HBM],
        out_specs=[VMEM, VMEM],
        out_shape=[
            jax.ShapeDtypeStruct((CAP, 8, FLAT), BF16),
            jax.ShapeDtypeStruct((CAP, 1, 8), jnp.int32),
        ],
        scratch_shapes=[pltpu.VMEM((WIDE // 128, got.shape[0], 128), F32)],
        compiler_params=pltpu.CompilerParams(vmem_limit_bytes=SMALL_VMEM),
        cost_estimate=pl.CostEstimate(flops=10**7, bytes_accessed=10**6, transcendentals=0),
        name="place_pages",
    )(got, follow)


def along_ctx(a, core0, core1=None):
    pairs = []
    for i in range(16):
        x, y, c = i // 4, i // 2 % 2, i % 2
        dx, dy, dc = core1 if c and core1 else core0
        pairs.append((i, (x + dx) % 4 * 4 + (y + dy) % 2 * 2 + (c + dc) % 2))
    return lax.ppermute(a, "ctx", pairs)


def per_device(ql, kv, qu, ka, vu, block_order, page_owner):
    ql, kv = ql[0], kv[0]
    own, cut = pack(block_order, page_owner[:, :, 0], kv)
    sibling = (0, 0, 1)
    y = along_ctx(own, (0, 1, 0))
    xp = along_ctx(own, (1, 0, 0))
    xm = along_ctx(own, (3, 0, 0))
    got = lax.all_to_all(cut.reshape(8, CAP * PAGE, WIDE), "prompt", 0, 0, tiled=True)
    got = got.reshape(8 * CAP * PAGE, WIDE)
    q, token = queries(block_order, ql, qu, ka, own)
    y, both, near = join([own, y, xp, xm], ((1,), (0, 1), (0, 1, 2, 3)), token)
    near_s = along_ctx(near, sibling)
    yxp = along_ctx(y, (1, 0, 0))
    yxm = along_ctx(y, (3, 0, 0))
    two = along_ctx(both, (2, 0, 0))
    state, token = attend(q, [near, near_s])
    (far,) = join([yxp, yxm, two], ((0, 1, 2),), token, got)
    far_s = along_ctx(far, sibling)
    cache, start = place_pages(got, token)
    out = attend(q, [far, far_s], state, vu, group=8)

    cache = jnp.transpose(cache, (1, 0, 2))[None, None]
    start = jnp.transpose(start, (1, 2, 0))[None]
    return out[None], cache, start


def solution(mesh):
    return jax.shard_map(
        per_device,
        mesh=mesh,
        in_specs=(
            P("prompt", "ctx", None),
            P("prompt", "ctx", None),
            P(),
            P(),
            P(),
            P("prompt", "ctx"),
            P("prompt", "ctx", None),
        ),
        out_specs=(
            P("prompt", "ctx", None),
            P("prompt", "ctx", None, None, None),
            P("prompt", "ctx", None, None),
        ),
        check_vma=False,
    )
```

```python
import functools
import math

import jax
import jax.numpy as jnp
import numpy as np
from jax import lax
from jax.experimental import pallas as pl
from jax.experimental.pallas import tpu as pltpu
from jax.sharding import PartitionSpec as P

F32 = jnp.float32
BF16 = jnp.bfloat16
NOPE, ROPE, KVR, VD, HEADS = 128, 64, 512, 128, 16
LAT = KVR + ROPE
WIDE = 640
PAGE, PAGES, CAP = 16, 12, 3
HALF, ROWS = 96, 192
BLOCKS = 32
FLAT = PAGE * LAT
BIG = 1e30
SCALE2 = (NOPE + ROPE) ** -0.5 * math.log2(math.e)
VMEM_LIMIT = 60 * 2**20
QUERY_VMEM = 60 * 2**20
ATTEND_VMEM = 52 * 2**20
SMALL_VMEM = 8 * 2**20
CHUNK = 512


def rope_tables():
    lane = np.arange(128)
    freq = 10000.0 ** (-2.0 * (lane % 32) / ROPE)
    sign = np.where(lane % 64 < 32, -1.0, 1.0)

    def table(places):
        angle = places[:, None] * freq
        return np.concatenate([np.cos(angle), sign * np.sin(angle)], axis=1).astype(np.float32)

    return table(np.arange(BLOCKS) * float(HALF)), table(np.arange(HALF) * 1.0)


def query_kernel(
    blk_h, ql_h, qu_h, ka_h, tab_h, _, out_h, token, blk, ql, qu, ka, tab, out, rope_s, ext_s, sem
):
    chunks = qu.shape[0]
    width = qu.shape[2]
    copies = [
        pltpu.make_async_copy(blk_h, blk, sem.at[0]),
        pltpu.make_async_copy(tab_h, tab, sem.at[1]),
        pltpu.make_async_copy(ql_h, ql, sem.at[2]),
    ]
    for j in range(chunks):
        part = qu_h.at[:, j * width : (j + 1) * width]
        copies.append(pltpu.make_async_copy(part, qu.at[j], sem.at[4 + j]))
    copies.insert(4, pltpu.make_async_copy(ka_h, ka, sem.at[3]))
    for copy in copies:
        copy.start()
    copies[0].wait()
    copies[1].wait()
    half_lane = lax.broadcasted_iota(jnp.int32, (HALF, 128), 1)
    for slot in range(2):
        here = blk[0, slot]
        base = tab[pl.ds(here, 1), :]
        bc, bs = base[:, :128], base[:, 128:]
        oc, os = tab[BLOCKS:, :128], tab[BLOCKS:, 128:]
        rows = slice(slot * HALF, (slot + 1) * HALF)
        rope_s[rows, :128] = bc * oc - bs * os
        rope_s[rows, 128:] = bs * oc + bc * os
        later = (half_lane >= 64 + here + 1) & (half_lane < 64 + BLOCKS)
        ext_s[rows, :] = jnp.where(later, -BIG, 0.0)
    lane = lax.broadcasted_iota(jnp.int32, (ROWS, 128), 1)
    low = lane < 64
    token[...] = jnp.zeros(token.shape, F32)
    copies[2].wait()
    outgoing = []
    for c in range(chunks):
        copies[3 if c == 0 else 4 + c].wait()
        both = jnp.dot(ql[...], qu[c], preferred_element_type=F32).astype(BF16)
        if c == 0:
            copies[4].wait()
        for j in range(width // 384):
            even, at = (c * width // 384 + j) * 2, 384 * j
            t0 = both[:, at : at + 128]
            t1 = both[:, at + 128 : at + 256].astype(F32)
            t2 = both[:, at + 256 : at + 384].astype(F32)
            odd = jnp.where(low, t2, t1).astype(BF16)
            pair = jnp.where(low, t1, t2)
            swapped = jnp.where(lane % 64 < 32, pltpu.roll(pair, 96, 1), pltpu.roll(pair, 32, 1))
            turned = pair * rope_s[:, :128] + swapped * rope_s[:, 128:]
            out[even, :, :KVR] = jnp.dot(t0, ka[even], preferred_element_type=F32).astype(BF16)
            odd_key = jnp.concatenate([ka[even + 1, 64:, :], ka[even + 1, :64, :]], axis=0)
            out[even + 1, :, :KVR] = jnp.dot(odd, odd_key, preferred_element_type=F32).astype(BF16)
            out[even, :, KVR:] = jnp.where(low, turned, ext_s[...]).astype(BF16)
            turned = pltpu.roll(turned, 64, 1)
            out[even + 1, :, KVR:] = jnp.where(low, turned, ext_s[...]).astype(BF16)
        heads = pl.ds(c * HEADS // chunks, HEADS // chunks)
        done = pltpu.make_async_copy(out.at[heads], out_h.at[heads], sem.at[4 + chunks + c])
        done.start()
        outgoing.append(done)
    for done in outgoing:
        done.wait()


HBM = pl.BlockSpec(memory_space=pltpu.HBM)
VMEM = pl.BlockSpec(memory_space=pltpu.VMEM)
TOKEN = jax.ShapeDtypeStruct((8, 128), F32)


def queries(blk, ql, qu, ka, follow, chunks=4):
    width = qu.shape[1] // chunks
    table = np.concatenate(rope_tables(), axis=0)
    return pl.pallas_call(
        query_kernel,
        in_specs=[HBM] * 6,
        out_specs=[HBM, VMEM],
        scratch_shapes=[
            pltpu.SMEM(blk.shape, jnp.int32),
            pltpu.VMEM(ql.shape, BF16),
            pltpu.VMEM((chunks, qu.shape[0], width), BF16),
            pltpu.VMEM(ka.shape, BF16),
            pltpu.VMEM(table.shape, F32),
            pltpu.VMEM((HEADS, ROWS, WIDE), BF16),
            pltpu.VMEM((ROWS, 256), F32),
            pltpu.VMEM((ROWS, 128), F32),
            pltpu.SemaphoreType.DMA((4 + 2 * chunks,)),
        ],
        out_shape=[jax.ShapeDtypeStruct((HEADS, ROWS, WIDE), BF16), TOKEN],
        compiler_params=pltpu.CompilerParams(vmem_limit_bytes=QUERY_VMEM),
        cost_estimate=pl.CostEstimate(
            flops=int(2.6e9), bytes_accessed=int(15e6), transcendentals=0
        ),
        name="queries",
    )(blk, ql, qu, ka, jnp.asarray(table), follow)


def join_kernel(count, groups, *refs):
    outs = refs[len(refs) - len(groups) :]
    for group, out in zip(groups, outs):
        at = 0
        for i in group:
            piece = refs[i]
            out[at : at + piece.shape[0], :] = piece[...]
            at += piece.shape[0]


def join(pieces, groups, *follow):
    rows = [sum(pieces[i].shape[0] for i in group) for group in groups]
    return pl.pallas_call(
        functools.partial(join_kernel, len(pieces), groups),
        in_specs=[VMEM] * len(pieces) + [HBM] * len(follow),
        out_specs=[VMEM] * len(groups),
        out_shape=[jax.ShapeDtypeStruct((n, WIDE), BF16) for n in rows],
        compiler_params=pltpu.CompilerParams(vmem_limit_bytes=SMALL_VMEM),
        cost_estimate=pl.CostEstimate(flops=0, bytes_accessed=10**6, transcendentals=0),
        name="join",
    )(*pieces, *follow)


def lanes(op, a):
    parts = [a[:, at : at + 128] for at in range(0, a.shape[1], 128)]
    while len(parts) > 1:
        pairs = [parts[i : i + 2] for i in range(0, len(parts), 2)]
        parts = [op(*pair) if len(pair) == 2 else pair[0] for pair in pairs]
    return parts[0]


def attend_kernel(sizes, group, first, last, follows, *refs):
    refs = list(refs)
    q_ref = refs.pop(0)
    pieces = [refs.pop(0) for _ in sizes]
    if follows:
        refs.pop(0)
    if not first:
        state_in = refs.pop(0)
    if last:
        up_ref, out_ref = refs.pop(0), refs.pop(0)
    else:
        state_out, token = refs.pop(0), refs.pop(0)
    keys = refs.pop(0)
    mask = refs.pop(0) if first else None
    pair = 2
    rows = pair * ROWS

    @pl.when(pl.program_id(0) == 0)
    def _():
        at = 0
        for size, piece in zip(sizes, pieces):
            keys[at : at + size, :] = piece[...]
            at += size
        if not last:
            token[...] = jnp.zeros(token.shape, F32)
        if first:
            r = lax.broadcasted_iota(jnp.int32, (ROWS, 256), 0)
            t = lax.broadcasted_iota(jnp.int32, (ROWS, 256), 1)
            same = ((r < HALF) & (t < HALF)) | ((r >= HALF) & (t >= HALF) & (t < ROWS))
            mask[...] = jnp.where(same & (t > r), -BIG, 0.0)

    def score(j):
        q = q_ref[j * pair : (j + 1) * pair].reshape(rows, WIDE)
        s = lax.dot_general(q, keys[...], (((1,), (1,)), ((), ())), preferred_element_type=F32)
        if first:
            head = (s[:, :256].reshape(pair, ROWS, 256) + mask[...]).reshape(rows, 256)
            s = jnp.concatenate([head, s[:, 256:]], axis=1)
        return s

    def finish(j, s):
        peak = jnp.max(lanes(jnp.maximum, s), axis=1, keepdims=True)
        here = slice(j * pair, (j + 1) * pair)
        if not first:
            marks = state_in[here, :, KVR:].reshape(rows, 128).astype(F32)
            old_peak = marks[:, 0:1] + marks[:, 1:2] + marks[:, 2:3]
            old_total = marks[:, 3:4] + marks[:, 4:5] + marks[:, 5:6]
            peak = jnp.maximum(peak, old_peak)
            shrink = jnp.exp2((old_peak - peak) * SCALE2)
        level = peak * SCALE2
        acc, total = None, None
        for at in range(0, s.shape[1], CHUNK):
            weights = jnp.exp2(s[:, at : at + CHUNK] * SCALE2 - level)
            part = lanes(jnp.add, weights)
            total = part if total is None else total + part
            part = jnp.dot(
                weights.astype(BF16), keys[at : at + CHUNK, :KVR], preferred_element_type=F32
            )
            acc = part if acc is None else acc + part
        total = jnp.sum(total, axis=1, keepdims=True)
        if not first:
            total = total + old_total * shrink
            acc = acc + state_in[here, :, :KVR].reshape(rows, KVR).astype(F32) * shrink
        if last:
            latent = (acc * (1.0 / total)).astype(BF16)
            for k in range(pair):
                h = j * pair + k
                out_ref[:, h * VD : (h + 1) * VD] = jnp.dot(
                    latent[k * ROWS : (k + 1) * ROWS], up_ref[h], preferred_element_type=F32
                ).astype(BF16)
        else:
            lane = lax.broadcasted_iota(jnp.int32, (rows, 128), 1)
            marks = jnp.zeros((rows, 128), F32)
            for base, rest in ((0, peak), (3, total)):
                for part in range(3):
                    top = rest.astype(BF16).astype(F32)
                    marks = jnp.where(lane == base + part, top, marks)
                    rest = rest - top
            state_out[here, :, KVR:] = marks.astype(BF16).reshape(pair, ROWS, 128)
            state_out[here, :, :KVR] = acc.astype(BF16).reshape(pair, ROWS, KVR)

    steps = group // pair
    s = score(0)
    for j in range(steps):
        after = score(j + 1) if j + 1 < steps else None
        finish(j, s)
        s = after


def attend(q, pieces, state=None, up=None, group=4, follow=None):
    pieces = [piece if isinstance(piece, tuple) else (piece, 0, piece.shape[0]) for piece in pieces]
    sizes = [size for _, _, size in pieces]
    first, last = state is None, up is not None
    span = sum(sizes)
    heads = lambda width: pl.BlockSpec((group, ROWS, width), lambda i: (i, 0, 0))
    in_specs = [heads(WIDE)] + [
        pl.BlockSpec((size, WIDE), lambda i, at=at: (at, 0)) for _, at, size in pieces
    ]
    args = [q, *(piece for piece, _, _ in pieces)]
    if follow is not None:
        in_specs.append(HBM)
        args.append(follow)
    if not first:
        in_specs.append(heads(WIDE))
        args.append(state)
    if last:
        in_specs.append(pl.BlockSpec((group, KVR, VD), lambda i: (i, 0, 0)))
        args.append(up)
        out_specs = pl.BlockSpec((ROWS, group * VD), lambda i: (0, i))
        out_shape = jax.ShapeDtypeStruct((ROWS, HEADS * VD), BF16)
    else:
        out_specs = [heads(WIDE), pl.BlockSpec((8, 128), lambda i: (0, 0))]
        out_shape = [
            jax.ShapeDtypeStruct((HEADS, ROWS, WIDE), BF16),
            TOKEN,
        ]
    scratch = [pltpu.VMEM((span, WIDE), BF16)]
    if first:
        scratch.append(pltpu.VMEM((ROWS, 256), F32))
    flops = 2 * HEADS * ROWS * span * (768 + KVR)
    return pl.pallas_call(
        functools.partial(attend_kernel, sizes, group, first, last, follow is not None),
        grid=(HEADS // group,),
        in_specs=in_specs,
        out_specs=out_specs,
        out_shape=out_shape,
        scratch_shapes=scratch,
        compiler_params=pltpu.CompilerParams(vmem_limit_bytes=ATTEND_VMEM),
        cost_estimate=pl.CostEstimate(
            flops=flops, bytes_accessed=int(16e6), transcendentals=HEADS * ROWS * span
        ),
        name="attend_first" if first else "attend_last" if last else "attend_next",
    )(*args)


def pack_kernel(blk_h, owners_h, kv_h, out, cut, blk, owners, kv, sem):
    copies = [
        pltpu.make_async_copy(blk_h, blk, sem.at[0]),
        pltpu.make_async_copy(owners_h, owners, sem.at[1]),
        pltpu.make_async_copy(kv_h, kv, sem.at[2]),
    ]
    for copy in copies:
        copy.start()
    cut[...] = jnp.zeros(cut.shape, BF16)
    row = lax.broadcasted_iota(jnp.int32, (ROWS, 128), 0)
    lane = lax.broadcasted_iota(jnp.int32, (ROWS, 128), 1)
    copies[0].wait()
    copies[1].wait()
    first = row < HALF
    marks = (lane == 64 + jnp.where(first, blk[0, 0], blk[0, 1])) | (
        lane == 64 + BLOCKS + jnp.where(first, row, row - HALF) // PAGE
    )
    copies[2].wait()
    out[:, :KVR] = kv[:, :KVR]
    tail = jnp.concatenate([kv[:, KVR:], jnp.zeros((ROWS, 64), BF16)], axis=1).astype(F32)
    out[:, KVR:] = jnp.where(marks, 1.0, tail).astype(BF16)
    for p in range(PAGES):
        owner = owners[0, p]
        rank = jnp.int32(0)
        for earlier in range(p):
            rank = rank + jnp.where(owners[0, earlier] == owner, 1, 0)
        at = pl.multiple_of((owner * CAP + rank) * PAGE, PAGE)
        cut[pl.ds(at, PAGE), :] = out[p * PAGE : (p + 1) * PAGE, :]


def pack(blk, owners, kv):
    return pl.pallas_call(
        pack_kernel,
        in_specs=[HBM, HBM, HBM],
        out_specs=[VMEM, VMEM],
        out_shape=[
            jax.ShapeDtypeStruct((ROWS, WIDE), BF16),
            jax.ShapeDtypeStruct((8 * CAP * PAGE, WIDE), BF16),
        ],
        scratch_shapes=[
            pltpu.SMEM(blk.shape, jnp.int32),
            pltpu.SMEM(owners.shape, jnp.int32),
            pltpu.VMEM(kv.shape, BF16),
            pltpu.SemaphoreType.DMA((3,)),
        ],
        compiler_params=pltpu.CompilerParams(vmem_limit_bytes=VMEM_LIMIT),
        cost_estimate=pl.CostEstimate(flops=10**5, bytes_accessed=10**6, transcendentals=0),
        name="pack",
    )(blk, owners, kv)


def place_kernel(got, _, out, start, wide):
    rows = CAP * PAGE
    for t in range(WIDE // 128):
        wide[t] = got[:, t * 128 : (t + 1) * 128].astype(F32)
    lane = lax.broadcasted_iota(jnp.int32, (8, 128), 1)
    eye = lax.broadcasted_iota(jnp.int32, (8, 128), 0) == lane
    is_block = (lane >= 64) & (lane < 64 + BLOCKS)
    is_page = (lane >= 64 + BLOCKS) & (lane < 70 + BLOCKS)
    place = jnp.where(is_block, (lane - 64) * HALF, (lane - 64 - BLOCKS) * PAGE).astype(F32)
    place = jnp.where(is_block | is_page, place, 0.0)
    for k in range(CAP):
        for r in range(0, PAGE, 2):
            pair = []
            for i in range(2):
                every = pl.ds(k * PAGE + r + i, 8, stride=rows)
                parts = [wide[t, every, :] for t in range(WIDE // 128)]
                pair.append(jnp.concatenate(parts, axis=1))
            if r == 0:
                mark = pair[0][:, KVR:]
                where = jnp.sum(mark * place, axis=1, keepdims=True)
                there = jnp.sum(jnp.where(is_block, mark, 0.0), axis=1, keepdims=True)
                where = jnp.where(there > 0.5, where, -1.0)
                where = jnp.sum(jnp.where(eye, where, 0.0), axis=0, keepdims=True)
                start[k] = where[:, :8].astype(jnp.int32)
            both = jnp.concatenate([pair[0][:, :LAT], pair[1][:, :LAT]], axis=1)
            out[k, :, r * LAT : (r + 2) * LAT] = both.astype(BF16)


def place_pages(got, follow):
    return pl.pallas_call(
        place_kernel,
        in_specs=[VMEM, HBM],
        out_specs=[VMEM, VMEM],
        out_shape=[
            jax.ShapeDtypeStruct((CAP, 8, FLAT), BF16),
            jax.ShapeDtypeStruct((CAP, 1, 8), jnp.int32),
        ],
        scratch_shapes=[pltpu.VMEM((WIDE // 128, got.shape[0], 128), F32)],
        compiler_params=pltpu.CompilerParams(vmem_limit_bytes=SMALL_VMEM),
        cost_estimate=pl.CostEstimate(flops=10**7, bytes_accessed=10**6, transcendentals=0),
        name="place_pages",
    )(got, follow)


def along_ctx(a, core0, core1=None):
    pairs = []
    for i in range(16):
        x, y, c = i // 4, i // 2 % 2, i % 2
        dx, dy, dc = core1 if c and core1 else core0
        pairs.append((i, (x + dx) % 4 * 4 + (y + dy) % 2 * 2 + (c + dc) % 2))
    return lax.ppermute(a, "ctx", pairs)


def per_device(ql, kv, qu, ka, vu, block_order, page_owner):
    ql, kv = ql[0], kv[0]
    own, cut = pack(block_order, page_owner[:, :, 0], kv)
    sibling = (0, 0, 1)
    y = along_ctx(own, (0, 1, 0))
    xp = along_ctx(own, (1, 0, 0))
    xm = along_ctx(own, (3, 0, 0))
    got = lax.all_to_all(cut.reshape(8, CAP * PAGE, WIDE), "prompt", 0, 0, tiled=True)
    got = got.reshape(8 * CAP * PAGE, WIDE)
    q, token = queries(block_order, ql, qu, ka, own)
    both, near = join([own, y, xp, xm], ((0, 1), (0, 1, 2, 3)), token)
    near_s = along_ctx(near, sibling)
    yxp = along_ctx(y, (1, 0, 0))
    yxm = along_ctx(y, (3, 0, 0))
    two = along_ctx(both, (2, 0, 0))
    state, token = attend(q, [near, near_s], group=8)
    (far,) = join([yxp, yxm, two], ((0, 1, 2),), token, got)
    far_s = along_ctx(far, sibling)
    cache, start = place_pages(got, token)
    out = attend(q, [far, far_s], state, vu, group=8)

    cache = jnp.transpose(cache, (1, 0, 2))[None, None]
    start = jnp.transpose(start, (1, 2, 0))[None]
    return out[None], cache, start


def solution(mesh):
    return jax.shard_map(
        per_device,
        mesh=mesh,
        in_specs=(
            P("prompt", "ctx", None),
            P("prompt", "ctx", None),
            P(),
            P(),
            P(),
            P("prompt", "ctx"),
            P("prompt", "ctx", None),
        ),
        out_specs=(
            P("prompt", "ctx", None),
            P("prompt", "ctx", None, None, None),
            P("prompt", "ctx", None, None),
        ),
        check_vma=False,
    )
```

```python
import functools
import math

import jax
import jax.numpy as jnp
import numpy as np
from jax import lax
from jax.experimental import pallas as pl
from jax.experimental.pallas import tpu as pltpu
from jax.sharding import PartitionSpec as P

F32 = jnp.float32
BF16 = jnp.bfloat16
NOPE, ROPE, KVR, VD, HEADS = 128, 64, 512, 128, 16
LAT = KVR + ROPE
WIDE = 640
PAGE, PAGES, CAP = 16, 12, 3
HALF, ROWS = 96, 192
BLOCKS = 32
FLAT = PAGE * LAT
BIG = 1e30
SCALE2 = (NOPE + ROPE) ** -0.5 * math.log2(math.e)
VMEM_LIMIT = 60 * 2**20
QUERY_VMEM = 60 * 2**20
ATTEND_VMEM = 52 * 2**20
SMALL_VMEM = 8 * 2**20
CHUNK = 512


def rope_tables():
    lane = np.arange(128)
    freq = 10000.0 ** (-2.0 * (lane % 32) / ROPE)
    sign = np.where(lane % 64 < 32, -1.0, 1.0)

    def table(places):
        angle = places[:, None] * freq
        return np.concatenate([np.cos(angle), sign * np.sin(angle)], axis=1).astype(np.float32)

    return table(np.arange(BLOCKS) * float(HALF)), table(np.arange(HALF) * 1.0)


def query_kernel(
    blk_h, ql_h, qu_h, ka_h, tab_h, _, out_h, token, blk, ql, qu, ka, tab, out, rope_s, ext_s, sem
):
    chunks = qu.shape[0]
    width = qu.shape[2]
    copies = [
        pltpu.make_async_copy(blk_h, blk, sem.at[0]),
        pltpu.make_async_copy(tab_h, tab, sem.at[1]),
        pltpu.make_async_copy(ql_h, ql, sem.at[2]),
    ]
    for j in range(chunks):
        part = qu_h.at[:, j * width : (j + 1) * width]
        copies.append(pltpu.make_async_copy(part, qu.at[j], sem.at[4 + j]))
    copies.insert(4, pltpu.make_async_copy(ka_h, ka, sem.at[3]))
    for copy in copies:
        copy.start()
    copies[0].wait()
    copies[1].wait()
    half_lane = lax.broadcasted_iota(jnp.int32, (HALF, 128), 1)
    for slot in range(2):
        here = blk[0, slot]
        base = tab[pl.ds(here, 1), :]
        bc, bs = base[:, :128], base[:, 128:]
        oc, os = tab[BLOCKS:, :128], tab[BLOCKS:, 128:]
        rows = slice(slot * HALF, (slot + 1) * HALF)
        rope_s[rows, :128] = bc * oc - bs * os
        rope_s[rows, 128:] = bs * oc + bc * os
        later = (half_lane >= 64 + here + 1) & (half_lane < 64 + BLOCKS)
        ext_s[rows, :] = jnp.where(later, -BIG, 0.0)
    lane = lax.broadcasted_iota(jnp.int32, (ROWS, 128), 1)
    low = lane < 64
    token[...] = jnp.zeros(token.shape, F32)
    copies[2].wait()
    outgoing = []
    for c in range(chunks):
        copies[3 if c == 0 else 4 + c].wait()
        both = jnp.dot(ql[...], qu[c], preferred_element_type=F32).astype(BF16)
        if c == 0:
            copies[4].wait()
        for j in range(width // 384):
            even, at = (c * width // 384 + j) * 2, 384 * j
            t0 = both[:, at : at + 128]
            t1 = both[:, at + 128 : at + 256].astype(F32)
            t2 = both[:, at + 256 : at + 384].astype(F32)
            odd = jnp.where(low, t2, t1).astype(BF16)
            pair = jnp.where(low, t1, t2)
            swapped = jnp.where(lane % 64 < 32, pltpu.roll(pair, 96, 1), pltpu.roll(pair, 32, 1))
            turned = pair * rope_s[:, :128] + swapped * rope_s[:, 128:]
            out[even, :, :KVR] = jnp.dot(t0, ka[even], preferred_element_type=F32).astype(BF16)
            odd_key = jnp.concatenate([ka[even + 1, 64:, :], ka[even + 1, :64, :]], axis=0)
            out[even + 1, :, :KVR] = jnp.dot(odd, odd_key, preferred_element_type=F32).astype(BF16)
            out[even, :, KVR:] = jnp.where(low, turned, ext_s[...]).astype(BF16)
            turned = pltpu.roll(turned, 64, 1)
            out[even + 1, :, KVR:] = jnp.where(low, turned, ext_s[...]).astype(BF16)
        heads = pl.ds(c * HEADS // chunks, HEADS // chunks)
        done = pltpu.make_async_copy(out.at[heads], out_h.at[heads], sem.at[4 + chunks + c])
        done.start()
        outgoing.append(done)
    for done in outgoing:
        done.wait()


HBM = pl.BlockSpec(memory_space=pltpu.HBM)
VMEM = pl.BlockSpec(memory_space=pltpu.VMEM)
TOKEN = jax.ShapeDtypeStruct((8, 128), F32)


def queries(blk, ql, qu, ka, follow, chunks=4):
    width = qu.shape[1] // chunks
    table = np.concatenate(rope_tables(), axis=0)
    return pl.pallas_call(
        query_kernel,
        in_specs=[HBM] * 6,
        out_specs=[HBM, VMEM],
        scratch_shapes=[
            pltpu.SMEM(blk.shape, jnp.int32),
            pltpu.VMEM(ql.shape, BF16),
            pltpu.VMEM((chunks, qu.shape[0], width), BF16),
            pltpu.VMEM(ka.shape, BF16),
            pltpu.VMEM(table.shape, F32),
            pltpu.VMEM((HEADS, ROWS, WIDE), BF16),
            pltpu.VMEM((ROWS, 256), F32),
            pltpu.VMEM((ROWS, 128), F32),
            pltpu.SemaphoreType.DMA((4 + 2 * chunks,)),
        ],
        out_shape=[jax.ShapeDtypeStruct((HEADS, ROWS, WIDE), BF16), TOKEN],
        compiler_params=pltpu.CompilerParams(vmem_limit_bytes=QUERY_VMEM),
        cost_estimate=pl.CostEstimate(
            flops=int(2.6e9), bytes_accessed=int(15e6), transcendentals=0
        ),
        name="queries",
    )(blk, ql, qu, ka, jnp.asarray(table), follow)


def join_kernel(count, groups, *refs):
    outs = refs[len(refs) - len(groups) :]
    for group, out in zip(groups, outs):
        at = 0
        for i in group:
            piece = refs[i]
            out[at : at + piece.shape[0], :] = piece[...]
            at += piece.shape[0]


def join(pieces, groups, *follow):
    rows = [sum(pieces[i].shape[0] for i in group) for group in groups]
    return pl.pallas_call(
        functools.partial(join_kernel, len(pieces), groups),
        in_specs=[VMEM] * len(pieces) + [HBM] * len(follow),
        out_specs=[VMEM] * len(groups),
        out_shape=[jax.ShapeDtypeStruct((n, WIDE), BF16) for n in rows],
        compiler_params=pltpu.CompilerParams(vmem_limit_bytes=SMALL_VMEM),
        cost_estimate=pl.CostEstimate(flops=0, bytes_accessed=10**6, transcendentals=0),
        name="join",
    )(*pieces, *follow)


def lanes(op, a):
    parts = [a[:, at : at + 128] for at in range(0, a.shape[1], 128)]
    while len(parts) > 1:
        pairs = [parts[i : i + 2] for i in range(0, len(parts), 2)]
        parts = [op(*pair) if len(pair) == 2 else pair[0] for pair in pairs]
    return parts[0]


def attend_kernel(sizes, group, first, last, follows, *refs):
    refs = list(refs)
    q_ref = refs.pop(0)
    pieces = [refs.pop(0) for _ in sizes]
    if follows:
        refs.pop(0)
    if not first:
        state_in = refs.pop(0)
    if last:
        up_ref, out_ref = refs.pop(0), refs.pop(0)
    else:
        state_out, token = refs.pop(0), refs.pop(0)
    keys = refs.pop(0)
    mask = refs.pop(0) if first else None
    pair = 2
    rows = pair * ROWS

    @pl.when(pl.program_id(0) == 0)
    def _():
        at = 0
        for size, piece in zip(sizes, pieces):
            keys[at : at + size, :] = piece[...]
            at += size
        if not last:
            token[...] = jnp.zeros(token.shape, F32)
        if first:
            r = lax.broadcasted_iota(jnp.int32, (ROWS, 256), 0)
            t = lax.broadcasted_iota(jnp.int32, (ROWS, 256), 1)
            same = ((r < HALF) & (t < HALF)) | ((r >= HALF) & (t >= HALF) & (t < ROWS))
            mask[...] = jnp.where(same & (t > r), -BIG, 0.0)

    def score(j):
        q = q_ref[j * pair : (j + 1) * pair].reshape(rows, WIDE)
        s = lax.dot_general(q, keys[...], (((1,), (1,)), ((), ())), preferred_element_type=F32)
        if first:
            head = (s[:, :256].reshape(pair, ROWS, 256) + mask[...]).reshape(rows, 256)
            s = jnp.concatenate([head, s[:, 256:]], axis=1)
        return s

    def finish(j, s):
        peak = jnp.max(lanes(jnp.maximum, s), axis=1, keepdims=True)
        here = slice(j * pair, (j + 1) * pair)
        if not first:
            marks = state_in[here, :, KVR:].reshape(rows, 128).astype(F32)
            old_peak = marks[:, 0:1] + marks[:, 1:2] + marks[:, 2:3]
            old_total = marks[:, 3:4] + marks[:, 4:5] + marks[:, 5:6]
            peak = jnp.maximum(peak, old_peak)
            shrink = jnp.exp2((old_peak - peak) * SCALE2)
        level = peak * SCALE2
        acc, total = None, None
        for at in range(0, s.shape[1], CHUNK):
            weights = jnp.exp2(s[:, at : at + CHUNK] * SCALE2 - level)
            part = lanes(jnp.add, weights)
            total = part if total is None else total + part
            part = jnp.dot(
                weights.astype(BF16), keys[at : at + CHUNK, :KVR], preferred_element_type=F32
            )
            acc = part if acc is None else acc + part
        total = jnp.sum(total, axis=1, keepdims=True)
        if not first:
            total = total + old_total * shrink
            acc = acc + state_in[here, :, :KVR].reshape(rows, KVR).astype(F32) * shrink
        if last:
            latent = (acc * (1.0 / total)).astype(BF16)
            for k in range(pair):
                h = j * pair + k
                out_ref[:, h * VD : (h + 1) * VD] = jnp.dot(
                    latent[k * ROWS : (k + 1) * ROWS], up_ref[h], preferred_element_type=F32
                ).astype(BF16)
        else:
            lane = lax.broadcasted_iota(jnp.int32, (rows, 128), 1)
            marks = jnp.zeros((rows, 128), F32)
            for base, rest in ((0, peak), (3, total)):
                for part in range(3):
                    top = rest.astype(BF16).astype(F32)
                    marks = jnp.where(lane == base + part, top, marks)
                    rest = rest - top
            state_out[here, :, KVR:] = marks.astype(BF16).reshape(pair, ROWS, 128)
            state_out[here, :, :KVR] = acc.astype(BF16).reshape(pair, ROWS, KVR)

    steps = group // pair
    s = score(0)
    for j in range(steps):
        after = score(j + 1) if j + 1 < steps else None
        finish(j, s)
        s = after


def attend(q, pieces, state=None, up=None, group=4, follow=None):
    pieces = [piece if isinstance(piece, tuple) else (piece, 0, piece.shape[0]) for piece in pieces]
    sizes = [size for _, _, size in pieces]
    first, last = state is None, up is not None
    span = sum(sizes)
    heads = lambda width: pl.BlockSpec((group, ROWS, width), lambda i: (i, 0, 0))
    in_specs = [heads(WIDE)] + [
        pl.BlockSpec((size, WIDE), lambda i, at=at: (at, 0)) for _, at, size in pieces
    ]
    args = [q, *(piece for piece, _, _ in pieces)]
    if follow is not None:
        in_specs.append(HBM)
        args.append(follow)
    if not first:
        in_specs.append(heads(WIDE))
        args.append(state)
    if last:
        in_specs.append(pl.BlockSpec((group, KVR, VD), lambda i: (i, 0, 0)))
        args.append(up)
        out_specs = pl.BlockSpec((ROWS, group * VD), lambda i: (0, i))
        out_shape = jax.ShapeDtypeStruct((ROWS, HEADS * VD), BF16)
    else:
        out_specs = [heads(WIDE), pl.BlockSpec((8, 128), lambda i: (0, 0))]
        out_shape = [
            jax.ShapeDtypeStruct((HEADS, ROWS, WIDE), BF16),
            TOKEN,
        ]
    scratch = [pltpu.VMEM((span, WIDE), BF16)]
    if first:
        scratch.append(pltpu.VMEM((ROWS, 256), F32))
    flops = 2 * HEADS * ROWS * span * (768 + KVR)
    return pl.pallas_call(
        functools.partial(attend_kernel, sizes, group, first, last, follow is not None),
        grid=(HEADS // group,),
        in_specs=in_specs,
        out_specs=out_specs,
        out_shape=out_shape,
        scratch_shapes=scratch,
        compiler_params=pltpu.CompilerParams(vmem_limit_bytes=ATTEND_VMEM),
        cost_estimate=pl.CostEstimate(
            flops=flops, bytes_accessed=int(16e6), transcendentals=HEADS * ROWS * span
        ),
        name="attend_first" if first else "attend_last" if last else "attend_next",
    )(*args)


def pack_kernel(blk_h, owners_h, kv_h, out, cut, blk, owners, kv, sem):
    copies = [
        pltpu.make_async_copy(blk_h, blk, sem.at[0]),
        pltpu.make_async_copy(owners_h, owners, sem.at[1]),
        pltpu.make_async_copy(kv_h, kv, sem.at[2]),
    ]
    for copy in copies:
        copy.start()
    cut[...] = jnp.zeros(cut.shape, BF16)
    row = lax.broadcasted_iota(jnp.int32, (ROWS, 128), 0)
    lane = lax.broadcasted_iota(jnp.int32, (ROWS, 128), 1)
    copies[0].wait()
    copies[1].wait()
    first = row < HALF
    marks = (lane == 64 + jnp.where(first, blk[0, 0], blk[0, 1])) | (
        lane == 64 + BLOCKS + jnp.where(first, row, row - HALF) // PAGE
    )
    copies[2].wait()
    out[:, :KVR] = kv[:, :KVR]
    tail = jnp.concatenate([kv[:, KVR:], jnp.zeros((ROWS, 64), BF16)], axis=1).astype(F32)
    out[:, KVR:] = jnp.where(marks, 1.0, tail).astype(BF16)
    for p in range(PAGES):
        owner = owners[0, p]
        rank = jnp.int32(0)
        for earlier in range(p):
            rank = rank + jnp.where(owners[0, earlier] == owner, 1, 0)
        at = pl.multiple_of((owner * CAP + rank) * PAGE, PAGE)
        cut[pl.ds(at, PAGE), :] = out[p * PAGE : (p + 1) * PAGE, :]


def pack(blk, owners, kv):
    return pl.pallas_call(
        pack_kernel,
        in_specs=[HBM, HBM, HBM],
        out_specs=[VMEM, VMEM],
        out_shape=[
            jax.ShapeDtypeStruct((ROWS, WIDE), BF16),
            jax.ShapeDtypeStruct((8 * CAP * PAGE, WIDE), BF16),
        ],
        scratch_shapes=[
            pltpu.SMEM(blk.shape, jnp.int32),
            pltpu.SMEM(owners.shape, jnp.int32),
            pltpu.VMEM(kv.shape, BF16),
            pltpu.SemaphoreType.DMA((3,)),
        ],
        compiler_params=pltpu.CompilerParams(vmem_limit_bytes=VMEM_LIMIT),
        cost_estimate=pl.CostEstimate(flops=10**5, bytes_accessed=10**6, transcendentals=0),
        name="pack",
    )(blk, owners, kv)


def place_kernel(got, _, out, start, wide):
    rows = CAP * PAGE
    for t in range(WIDE // 128):
        wide[t] = got[:, t * 128 : (t + 1) * 128].astype(F32)
    lane = lax.broadcasted_iota(jnp.int32, (8, 128), 1)
    eye = lax.broadcasted_iota(jnp.int32, (8, 128), 0) == lane
    is_block = (lane >= 64) & (lane < 64 + BLOCKS)
    is_page = (lane >= 64 + BLOCKS) & (lane < 70 + BLOCKS)
    place = jnp.where(is_block, (lane - 64) * HALF, (lane - 64 - BLOCKS) * PAGE).astype(F32)
    place = jnp.where(is_block | is_page, place, 0.0)
    for k in range(CAP):
        for r in range(0, PAGE, 2):
            pair = []
            for i in range(2):
                every = pl.ds(k * PAGE + r + i, 8, stride=rows)
                parts = [wide[t, every, :] for t in range(WIDE // 128)]
                pair.append(jnp.concatenate(parts, axis=1))
            if r == 0:
                mark = pair[0][:, KVR:]
                where = jnp.sum(mark * place, axis=1, keepdims=True)
                there = jnp.sum(jnp.where(is_block, mark, 0.0), axis=1, keepdims=True)
                where = jnp.where(there > 0.5, where, -1.0)
                where = jnp.sum(jnp.where(eye, where, 0.0), axis=0, keepdims=True)
                start[k] = where[:, :8].astype(jnp.int32)
            both = jnp.concatenate([pair[0][:, :LAT], pair[1][:, :LAT]], axis=1)
            out[k, :, r * LAT : (r + 2) * LAT] = both.astype(BF16)


def place_pages(got, follow):
    return pl.pallas_call(
        place_kernel,
        in_specs=[VMEM, HBM],
        out_specs=[VMEM, VMEM],
        out_shape=[
            jax.ShapeDtypeStruct((CAP, 8, FLAT), BF16),
            jax.ShapeDtypeStruct((CAP, 1, 8), jnp.int32),
        ],
        scratch_shapes=[pltpu.VMEM((WIDE // 128, got.shape[0], 128), F32)],
        compiler_params=pltpu.CompilerParams(vmem_limit_bytes=SMALL_VMEM),
        cost_estimate=pl.CostEstimate(flops=10**7, bytes_accessed=10**6, transcendentals=0),
        name="place_pages",
    )(got, follow)


def along_ctx(a, dx=0, dy=0, dc=0, flip=0):
    pairs = []
    for i in range(16):
        x, y, c = i // 4, i // 2 % 2, i % 2
        pairs.append((i, ((x ^ flip) + dx) % 4 * 4 + (y + dy) % 2 * 2 + (c + dc) % 2))
    return lax.ppermute(a, "ctx", pairs)


def per_device(ql, kv, qu, ka, vu, block_order, page_owner):
    ql, kv = ql[0], kv[0]
    own, cut = pack(block_order, page_owner[:, :, 0], kv)
    y = along_ctx(own, dy=1)
    xp = along_ctx(own, dx=1)
    xm = along_ctx(own, dx=3)
    got = lax.all_to_all(cut.reshape(8, CAP * PAGE, WIDE), "prompt", 0, 0, tiled=True)
    got = got.reshape(8 * CAP * PAGE, WIDE)
    q, token = queries(block_order, ql, qu, ka, own)
    both, near = join([own, y, xp, xm], ((0, 1), (0, 1, 2, 3)), token)
    near_s = along_ctx(near, dc=1)
    yx1 = along_ctx(y, flip=1)
    yx3 = along_ctx(y, flip=3)
    two = along_ctx(both, flip=2)
    state, token = attend(q, [near, near_s], group=8)
    (far,) = join([yx1, yx3, two], ((0, 1, 2),), token, got)
    far_s = along_ctx(far, dc=1)
    cache, start = place_pages(got, token)
    out = attend(q, [far, far_s], state, vu, group=8)

    cache = jnp.transpose(cache, (1, 0, 2))[None, None]
    start = jnp.transpose(start, (1, 2, 0))[None]
    return out[None], cache, start


def solution(mesh):
    return jax.shard_map(
        per_device,
        mesh=mesh,
        in_specs=(
            P("prompt", "ctx", None),
            P("prompt", "ctx", None),
            P(),
            P(),
            P(),
            P("prompt", "ctx"),
            P("prompt", "ctx", None),
        ),
        out_specs=(
            P("prompt", "ctx", None),
            P("prompt", "ctx", None, None, None),
            P("prompt", "ctx", None, None),
        ),
        check_vma=False,
    )
```
